32 devices in a mesh: dp: 4 (over y, core), row: 4 (over z), col: 2 (over x).
Axes of the slice: x: 2, y: 2, z: 4, core: 2. Of those that a mesh axis runs over, the one named last changes fastest.
Arguments:
- tokens: bfloat16 [4096, 2048], P(('dp', 'row', 'col')), may hold values from -6 to 6
- cotangent: bfloat16 [4096, 2048], P(('dp', 'row', 'col')), may hold values from -6 to 6
- w_query: bfloat16 [2048, 2048], P(('dp', 'row', 'col')), may hold values from -0.125 to 0.125
- w_keyval: bfloat16 [2048, 256], P(('dp', 'row', 'col')), may hold values from -0.125 to 0.125
- w_out: bfloat16 [2048, 2048], P(('dp', 'row', 'col')), may hold values from -1 to 1
- norm_attn: bfloat16 [2048], P(('dp', 'row', 'col')), may hold values from 0.25 to 1.75
- norm_ffn: bfloat16 [2048], P(('dp', 'row', 'col')), may hold values from 0.25 to 1.75
- w_gate: bfloat16 [2048, 6144], P('col', 'row'), may hold values from -0.125 to 0.125
- w_up: bfloat16 [2048, 6144], P('col', 'row'), may hold values from -0.125 to 0.125
- w_down: bfloat16 [6144, 2048], P('row', 'col'), may hold values from -0.078125 to 0.078125
- lengths: int32 [4, 4], P('dp'), may hold values from 1 to 512, 960 in all within a row
- placement: int32 [4, 4], P('dp'), may hold values from 0 to 3, each once within a row
Outputs:
- result: bfloat16 [4096, 2048], P(('dp', 'row'), 'col')
- grad_tokens: bfloat16 [4096, 2048], P(('dp', 'row', 'col'))
- grad_query: float32 [2048, 2048], P(('dp', 'row', 'col'))
- grad_keyval: float32 [2048, 256], P(('dp', 'row', 'col'))
- grad_out: float32 [2048, 2048], P(('dp', 'row', 'col'))
- grad_norm_attn: float32 [2048], P(('dp', 'row', 'col'))
- grad_norm_ffn: float32 [2048], P(('dp', 'row', 'col'))
- grad_gate: float32 [2048, 6144], P('col', 'row')
- grad_up: float32 [2048, 6144], P('col', 'row')
- grad_down: float32 [6144, 2048], P('row', 'col')
The draws below stay inside these ranges and needn't reach their ends.
Inputs may be any that keep to these rules, and one draw needn't show every extreme that they name: In each row the 4 lengths sum to 960, and the largest is exactly 512. `placement`: each row names every sequence of its group once.
All inputs are finite; a program needn't handle non-finite values.
Results may differ from the reference program's by a relative error of at most 0.019.
Values may be sent and summed in bfloat16 or wider, within the bound.
No kernel may reach another device: no remote copies, remote signals or barrier semaphores. Data moves between devices by JAX's collectives and lax.ppermute only.
A program may use at most 192 MiB of HBM per device.

```python
import math
import jax
import jax.numpy as jnp
import numpy as np
from jax import lax

D = 2048
HEADS = 16
HEAD = 128
FF = 6144
WINDOW = 1024
GROUP = 1024
TOKENS = 4096
LONGEST = 512
NSEQ = 4
PAD = 64
N_DP = 4


def shard_levels(own_key, extent, split, low, top_value):
    def one(position, parts):
        heights = jax.random.uniform(jax.random.fold_in(jax.random.fold_in(own_key, 6), position), (parts,), jnp.float32, low / len(split), top_value / len(split))
        return jnp.repeat(jnp.exp(heights), extent[position] // parts).reshape((-1,) + (1,) * (len(extent) - position - 1))

    level = one(*split[0])
    for cut in split[1:]:
        level = level * one(*cut)
    return level


def length_profile(count, total, limit, skew):
    weights = [(1 << 20) // math.isqrt(rank ** skew) + 1 for rank in range(2, count + 1)]
    rest, counts = total - limit - (count - 1), [1] * (count - 1)
    while rest > 0:
        candidates = [i for i in range(count - 1) if counts[i] < limit]
        whole, remaining = sum([weights[i] for i in candidates]), rest
        for i in candidates:
            addition = min(limit - counts[i], max(1, remaining * weights[i] // whole), rest)
            counts[i] = counts[i] + addition
            rest = rest - addition
    return np.array([limit] + counts)


def uneven_parts(rng, number_of, total, limit, skew):
    if number_of == 2:
        one = jax.random.randint(rng, (), max(1, total - limit), min(limit, total - 1) + 1)
        return jnp.stack([one, total - one])
    sizes = jnp.asarray(length_profile(number_of, total, limit, skew), jnp.int32)
    twos = (number_of - 1) // 2
    giver, sink = sizes[1:1 + 2 * twos:2], sizes[2:2 + 2 * twos:2]
    margin = jnp.minimum(giver - 1, limit - sink)
    shifted = jax.random.randint(jax.random.fold_in(rng, 1), (twos,), 0, 1 << 20) % (margin + 1)
    sizes = sizes.at[1:1 + 2 * twos:2].set(giver - shifted).at[2:2 + 2 * twos:2].set(sink + shifted)
    return sizes[jax.random.permutation(jax.random.fold_in(rng, 2), number_of)]


def bell_draw(rng, shape, deviation, reach, shards=(), kind=jnp.bfloat16):
    entries = jax.random.normal(rng, shape, jnp.float32) * deviation
    if len(shards) > 0:
        entries = shard_levels(rng, shape, shards, -0.22, 0.18) * entries
    return jnp.clip(entries, min=-reach, max=reach).astype(kind)


def setup_inputs(seed: int = 0) -> dict:
    key_of = jax.random.split(jax.random.key(seed), 13)
    return {
        "tokens": bell_draw(key_of[0], (TOKENS, D), 1.0, 6.0, ((0, 32),)),
        "cotangent": bell_draw(key_of[1], (TOKENS, D), 1.0, 6.0, ((0, 32),)),
        "w_query": bell_draw(key_of[2], (D, HEADS * HEAD), D ** -0.5, 0.125, ((0, 32),)),
        "w_keyval": bell_draw(key_of[3], (D, 2 * HEAD), D ** -0.5, 0.125, ((0, 32),)),
        "w_out": bell_draw(key_of[4], (HEADS * HEAD, D), (HEADS * HEAD // 64) ** -0.5, 1.0, ((0, 32),)),
        "norm_attn": jnp.clip(1.0 + 0.15 * jax.random.normal(key_of[5], (D,), jnp.float32), 0.25, 1.75).astype(jnp.bfloat16),
        "norm_ffn": jnp.clip(1.0 + 0.15 * jax.random.normal(key_of[6], (D,), jnp.float32), 0.25, 1.75).astype(jnp.bfloat16),
        "w_gate": bell_draw(key_of[7], (D, FF), D ** -0.5, 0.125, ((0, 2), (1, 4))),
        "w_up": bell_draw(key_of[8], (D, FF), D ** -0.5, 0.125, ((0, 2), (1, 4))),
        "w_down": bell_draw(key_of[9], (FF, D), FF ** -0.5, 0.078125, ((0, 4), (1, 2))),
        "lengths": jax.vmap(lambda own: uneven_parts(own, NSEQ, GROUP - PAD, LONGEST, 2))(jax.random.split(key_of[10], N_DP)).reshape((N_DP, NSEQ)).astype(jnp.int32),
        "placement": jax.vmap(lambda own: jax.random.permutation(own, NSEQ))(jax.random.split(key_of[11], N_DP)).reshape((N_DP, NSEQ)).astype(jnp.int32),
    }


EPSILON = 1e-06
ROPE_BASE = 10000.0
NEG_FILL = -1e+30

@jax.custom_vjp
def low(v):
    return lax.optimization_barrier(v.astype(jnp.bfloat16)).astype(jnp.float32)

@jax.custom_vjp
def low_back(v):
    return v

def low_keep(v):
    return (low(v), None)

def low_pass(kept, grad):
    return (grad,)

def back_keep(v):
    return (v, None)

def back_low(kept, grad):
    return (low(grad),)
low.defvjp(low_keep, low_pass)
low_back.defvjp(back_keep, back_low)

def exact_dot(left_side, right_side):
    return jnp.dot(left_side, right_side, precision=lax.Precision.HIGHEST)

def rms_norm(values, gain_vec):
    return values * lax.rsqrt(lax.optimization_barrier(jnp.mean(values * values, axis=-1, keepdims=True)) + EPSILON) * gain_vec

def rotate(values, offset):
    half_width = values.shape[-1] // 2
    frequency = ROPE_BASE ** (-2.0 * jnp.arange(half_width, dtype=jnp.float32) / values.shape[-1])
    angles = offset.astype(jnp.float32)[:, None] * frequency[None, :]
    angles = angles.reshape((values.shape[0],) + (1,) * (values.ndim - 2) + (half_width,))
    cos_part = jnp.cos(angles)
    sin_part = jnp.sin(angles)
    lower_half = values[..., :half_width]
    upper_half = values[..., half_width:]
    return jnp.concatenate([lower_half * cos_part - upper_half * sin_part, upper_half * cos_part + lower_half * sin_part], axis=-1)

def token_layout(length_row, order_row, first_row, row_count):
    seq_count = length_row.shape[0]
    slot_ids = jnp.arange(seq_count, dtype=jnp.int32)
    placed = lax.optimization_barrier(jnp.sum(jnp.where(order_row[:, None] == slot_ids[None, :], length_row[None, :], 0), axis=1, dtype=jnp.int32))
    seq_ends = jnp.cumsum(placed, dtype=jnp.int32)
    starts = seq_ends - placed
    where_at = first_row + jnp.arange(row_count, dtype=jnp.int32)
    slot_of = lax.optimization_barrier(jnp.sum((where_at[:, None] >= seq_ends[None, :]).astype(jnp.int32), axis=1, dtype=jnp.int32))
    seq_begin = lax.optimization_barrier(jnp.sum(jnp.where(slot_of[:, None] == slot_ids[None, :], starts[None, :], 0), axis=1, dtype=jnp.int32))
    inside = slot_of < seq_count
    segment = jnp.where(inside, slot_of, seq_count + where_at)
    segment = jnp.where(where_at < 0, -1, segment)
    offset = jnp.where(inside, where_at - seq_begin, 0)
    return (segment, where_at, offset)

def attend_group(queries, keyvals, segment, where_at):
    group_rows = queries.shape[0]
    block_rows = math.gcd(512, group_rows)
    key_pad = jnp.concatenate([jnp.zeros((WINDOW, keyvals.shape[1]), keyvals.dtype), keyvals], axis=0)
    seg_pad = jnp.concatenate([jnp.full((WINDOW,), -1, jnp.int32), segment])
    at_pad = jnp.concatenate([jnp.arange(-WINDOW, 0, dtype=jnp.int32), where_at])

    def one_block(block_id):
        row_start = (block_id * block_rows).astype(jnp.int32)
        query_blk = lax.dynamic_slice_in_dim(queries, row_start, block_rows, 0)
        seg_query = lax.dynamic_slice_in_dim(segment, row_start, block_rows, 0)
        at_query = lax.dynamic_slice_in_dim(where_at, row_start, block_rows, 0)
        key_blk = lax.dynamic_slice_in_dim(key_pad, row_start, block_rows + WINDOW, 0)
        seg_key = lax.dynamic_slice_in_dim(seg_pad, row_start, block_rows + WINDOW, 0)
        at_key = lax.dynamic_slice_in_dim(at_pad, row_start, block_rows + WINDOW, 0)
        scores = low_back(jnp.einsum('qhd,kd->hqk', query_blk, key_blk[:, :HEAD], precision=lax.Precision.HIGHEST))
        allowed = (seg_key[None, :] == seg_query[:, None]) & (at_key[None, :] <= at_query[:, None])
        masked = jnp.where(allowed[None], scores, NEG_FILL)
        row_peak = lax.optimization_barrier(jnp.max(masked, axis=-1, keepdims=True))
        expo_vals = jnp.where(allowed[None], jnp.exp(masked - row_peak), 0.0)
        weights_f = expo_vals / lax.optimization_barrier(jnp.sum(expo_vals, axis=-1, keepdims=True))
        return jnp.einsum('hqk,kd->qhd', low(weights_f), key_blk[:, HEAD:], precision=lax.Precision.HIGHEST)
    mixed = lax.map(jax.checkpoint(one_block), jnp.arange(group_rows // block_rows, dtype=jnp.int32))
    return mixed.reshape(group_rows, HEADS * HEAD)

def block_forward(values, params, segment, where_at, offset):
    w_query, w_keyval, w_out, gain_attn, gain_ffn, w_gate, w_up, w_down = params
    group_rows = values.shape[0]
    attn_in = low(rms_norm(values, gain_attn))
    query_raw = low_back(exact_dot(attn_in, w_query))
    keyval_raw = low_back(exact_dot(attn_in, w_keyval))
    queries = low(rotate(query_raw.reshape(group_rows, HEADS, HEAD), offset) * (1.0 / math.sqrt(HEAD)))
    keyvals = low(jnp.concatenate([rotate(keyval_raw[:, :HEAD], offset), keyval_raw[:, HEAD:]], axis=1))
    mixed = low(low_back(attend_group(queries, keyvals, segment, where_at)))
    branch = low(low_back(exact_dot(mixed, w_out)))
    resid = values + branch
    ffn_in = low(low_back(rms_norm(resid, gain_ffn)))
    gate_act = low_back(exact_dot(ffn_in, w_gate))
    up_act = low_back(exact_dot(ffn_in, w_up))
    hidden = low(jax.nn.gelu(gate_act, approximate=True) * up_act)
    return resid + exact_dot(hidden, w_down)

def reference(tokens, cotangent, w_query, w_keyval, w_out, norm_attn, norm_ffn, w_gate, w_up, w_down, lengths, placement):
    weights_all = (w_query.astype(jnp.float32), w_keyval.astype(jnp.float32), w_out.astype(jnp.float32), norm_attn.astype(jnp.float32), norm_ffn.astype(jnp.float32), w_gate.astype(jnp.float32), w_up.astype(jnp.float32), w_down.astype(jnp.float32))

    def one_group(carried, group_id):
        row_start = (group_id * GROUP).astype(jnp.int32)
        group_in = lax.dynamic_slice_in_dim(tokens, row_start, GROUP, 0).astype(jnp.float32)
        group_cot = lax.dynamic_slice_in_dim(cotangent, row_start, GROUP, 0).astype(jnp.float32)
        length_row = lax.dynamic_index_in_dim(lengths, group_id, 0, keepdims=False)
        order_row = lax.dynamic_index_in_dim(placement, group_id, 0, keepdims=False)
        segment, where_at, offset = token_layout(length_row, order_row, 0, GROUP)

        def forward(group_vals, params):
            return block_forward(group_vals, params, segment, where_at, offset)
        produced, pull_back = jax.vjp(forward, group_in, weights_all)
        input_grad, param_grads = pull_back(group_cot)
        carried = tuple((running + grad_piece for running, grad_piece in zip(carried, param_grads)))
        return (carried, (produced.astype(jnp.bfloat16), input_grad.astype(jnp.bfloat16)))
    start_sums = tuple((jnp.zeros(weight_arr.shape, jnp.float32) for weight_arr in weights_all))
    grad_sums, (out_rows, grad_rows) = lax.scan(one_group, start_sums, jnp.arange(N_DP, dtype=jnp.int32))
    return (out_rows.reshape(TOKENS, D), grad_rows.reshape(TOKENS, D), grad_sums[0], grad_sums[1], grad_sums[2], grad_sums[3], grad_sums[4], grad_sums[5], grad_sums[6], grad_sums[7])
```

```python
import functools
import math

import jax
import jax.numpy as jnp
from jax import lax
from jax.experimental import pallas as pl
from jax.experimental.pallas import tpu as pltpu
from jax.sharding import PartitionSpec as P

HEADS = 16
HEAD = 128

EPSILON = 1e-06
ROPE_BASE = 10000.0
NEG_FILL = -1e30
SCALE = 1.0 / math.sqrt(HEAD)
DP = ("y", "core")
EVERY = ("y", "core", "row", "col")
F32 = jnp.float32
BF16 = jnp.bfloat16
MIB = 2**20


def swap_core(value):
    return lax.ppermute(value, "core", [(0, 1), (1, 0)])


def swap_y(value, k):
    return lax.ppermute(value, "y", [(i, i ^ k) for i in range(lax.axis_size("y"))])


def swap_col(value):
    return lax.ppermute(value, "col", [(0, 1), (1, 0)])


def deal(value, axes):
    return lax.all_to_all(value, axes, split_axis=0, concat_axis=0, tiled=True)


def transpose_devices(value):
    n_dp, n_row, n_col = 2 * lax.axis_size("y"), lax.axis_size("row"), lax.axis_size("col")
    pairs = [
        ((d * n_row + r) * n_col + c, (r * n_row + d) * n_col + c)
        for d in range(n_dp)
        for r in range(n_row)
        for c in range(n_col)
    ]
    return lax.ppermute(value, EVERY, pairs)


def after(value, *others):
    return lax.optimization_barrier((value,) + others)[0]


def dot(left, right):
    return jnp.dot(left, right, preferred_element_type=F32)


def dot_tn(left, right):
    return lax.dot_general(left, right, (((0,), (0,)), ((), ())), preferred_element_type=F32)


def dot_nt(left, right):
    return lax.dot_general(left, right, (((1,), (1,)), ((), ())), preferred_element_type=F32)


def inv_rms(values):
    return lax.rsqrt(jnp.mean(values * values, axis=-1, keepdims=True) + EPSILON)


def run(body, ids, args, in_specs, outs, out_specs, grid=(1,), scratch=(), limit=56):
    def place(spec, array):
        if spec is None:
            zeros = (0,) * len(array.shape)
            return pl.BlockSpec(array.shape, lambda *_: zeros)
        return spec

    in_specs = [place(s, a) for s, a in zip(in_specs, args)]
    out_specs = [place(s, a) for s, a in zip(out_specs, outs)]
    return pl.pallas_call(
        body,
        grid_spec=pltpu.PrefetchScalarGridSpec(
            num_scalar_prefetch=1,
            grid=grid,
            in_specs=in_specs,
            out_specs=out_specs,
            scratch_shapes=list(scratch),
        ),
        out_shape=outs,
        compiler_params=pltpu.CompilerParams(
            vmem_limit_bytes=limit * MIB, dimension_semantics=("arbitrary",) * len(grid)
        ),
        cost_estimate=pl.CostEstimate(flops=0, bytes_accessed=10**5, transcendentals=0),
    )(ids, *args)


def sds(shape, dtype=BF16):
    return jax.ShapeDtypeStruct(shape, dtype)


def turn(values, cos_part, sin_part):
    return values * cos_part + pltpu.roll(values, HEAD // 2, 1) * sin_part


def cut_body(ids, g_ref, u_ref, d_ref, g_out, u_out, d_out):
    g_out[...] = g_ref[...]
    u_out[...] = u_ref[...]
    d_out[...] = d_ref[...]


def pack_body(n_row, ids, wq_ref, wkv_ref, ga_ref, gf_ref, out_ref):
    shard, kv = wkv_ref.shape
    hcols = wq_ref.shape[1] // n_row
    used = hcols + kv
    for r in range(n_row):
        out_ref[r, :shard, :hcols] = wq_ref[:, r * hcols : (r + 1) * hcols]
        out_ref[r, :shard, hcols:] = wkv_ref[...]
        line = lax.broadcasted_iota(jnp.int32, (16, used), 0)
        ga = jnp.broadcast_to(ga_ref[...].astype(F32), (16, used))
        gf = jnp.broadcast_to(gf_ref[...].astype(F32), (16, used))
        tail = jnp.where(line == 0, ga, jnp.where(line == 1, gf, 0.0))
        out_ref[r, shard:, :] = tail.astype(BF16)


def front_body(n_row, n_col, hcols, shard, ids, x_ref, own_ref, oth_ref, cos_ref, sin_ref, *refs):
    a_ref, kv_ref, q_ref, w_ref, gain_ref, g0, g1 = refs
    core = ids[0] & 1
    tall = shard + 16
    width = a_ref.shape[1]
    for flip, pack in ((0, own_ref), (1, oth_ref)):
        for p in range(pack.shape[0]):
            y, c = p // n_col, p % n_col
            for z in range(n_row):
                place = ((y * 2 + (core ^ flip)) * n_row + z) * n_col + c
                rows = pl.ds(pl.multiple_of(place * shard, shard), shard)
                w_ref[rows, :] = pack[p, z * tall : z * tall + shard, :]
                tail = pack[p, z * tall + shard : (z + 1) * tall, :HEAD].astype(F32)
                g0[pl.ds(place, 1), :] = tail[0:1]
                g1[pl.ds(place, 1), :] = tail[1:2]
    count = width // shard
    pick = lax.broadcasted_iota(jnp.int32, (HEAD, width), 0)
    feature = lax.broadcasted_iota(jnp.int32, (HEAD, width), 1)
    spread = ((feature & (shard - 1)) == pick).astype(F32)
    home = lax.broadcasted_iota(jnp.int32, (count, width), 0)
    mine = (lax.broadcasted_iota(jnp.int32, (count, width), 1) & ~(shard - 1)) == home * shard
    lines = []
    for g in (g0, g1):
        wide = jnp.dot(g[...], spread, preferred_element_type=F32)
        lines.append(jnp.sum(jnp.where(mine, wide, 0.0), axis=0, keepdims=True))
    gain = lines[0]
    gain_ref[...] = jnp.concatenate(lines * 4, axis=0)
    rows_all = x_ref.shape[0]
    step = 128
    for r in range(rows_all // step):
        rows = slice(r * step, (r + 1) * step)
        x = x_ref[rows, :].astype(F32)
        a_ref[rows, :] = (x * inv_rms(x) * gain).astype(BF16)
    kv = dot(a_ref[...], w_ref[:, hcols:])
    key = turn(kv[:, :HEAD], cos_ref[...], sin_ref[...])
    kv_ref[:, :HEAD] = key.astype(BF16)
    kv_ref[:, HEAD:] = kv[:, HEAD:].astype(BF16)
    raw = dot(a_ref[...], w_ref[:, :hcols])
    for h in range(hcols // HEAD):
        cols = slice(h * HEAD, (h + 1) * HEAD)
        q_ref[:, cols] = (turn(raw[:, cols], cos_ref[...], sin_ref[...]) * SCALE).astype(BF16)


def stack_heads(block, heads):
    return jnp.concatenate([block[:, h * HEAD : (h + 1) * HEAD] for h in range(heads)], axis=0)


def key_masks(lo, hi, count, n, n_col, col):
    j = lax.broadcasted_iota(jnp.int32, (1, count), 1)
    at = j + (j - (j & (n - 1))) * (n_col - 1)
    own, oth = at + col * n, at + (1 - col) * n
    return (own >= lo) & (own <= hi), (oth >= lo) & (oth <= hi)


def attend_body(n_row, n_col, heads, ids, q_ref, own_ref, oth_ref, lo_ref, hi_ref, m_ref, l_ref):
    col = ids[2]
    n = q_ref.shape[0] // n_row
    for r in range(n_row):
        rows = slice(r * n, (r + 1) * n)
        count = (r + 1) * n
        q = stack_heads(q_ref[rows, :], heads)
        lo = jnp.concatenate([lo_ref[rows, :]] * heads, axis=0)
        hi = jnp.concatenate([hi_ref[rows, :]] * heads, axis=0)
        ok_own, ok_oth = key_masks(lo, hi, count, n, n_col, col)
        s_own = jnp.where(ok_own, dot_nt(q, own_ref[:count, :HEAD]), NEG_FILL)
        s_oth = jnp.where(ok_oth, dot_nt(q, oth_ref[:count, :HEAD]), NEG_FILL)
        peak = jnp.maximum(
            jnp.max(s_own, axis=-1, keepdims=True), jnp.max(s_oth, axis=-1, keepdims=True)
        )
        e_own = jnp.where(ok_own, jnp.exp(s_own - peak), 0.0)
        e_oth = jnp.where(ok_oth, jnp.exp(s_oth - peak), 0.0)
        total = jnp.sum(e_own, axis=-1, keepdims=True) + jnp.sum(e_oth, axis=-1, keepdims=True)
        share = 1.0 / total
        mixed = dot((e_own * share).astype(BF16), own_ref[:count, HEAD:]) + dot(
            (e_oth * share).astype(BF16), oth_ref[:count, HEAD:]
        )
        for h in range(heads):
            m_ref[rows, h * HEAD : (h + 1) * HEAD] = mixed[h * n : (h + 1) * n].astype(BF16)
        log_total = peak + jnp.log(total)
        for h in range(heads):
            l_ref[rows, h : h + 1] = log_total[h * n : (h + 1) * n]


def branch_body(n_col, ids, mixed_ref, own_ref, oth_ref, part_ref, w_ref):
    core = ids[0] & 1
    shard = own_ref.shape[1]
    for flip, piece in ((0, own_ref), (1, oth_ref)):
        for p in range(piece.shape[0]):
            place = ((p // n_col) * 2 + (core ^ flip)) * n_col + p % n_col
            rows = pl.ds(pl.multiple_of(place * shard, shard), shard)
            w_ref[rows, :] = piece[p]
    part_ref[...] = dot(mixed_ref[...], w_ref[...]).astype(BF16)


def norm_body(ids, x_ref, branch_ref, gain_ref, f_ref):
    resid = x_ref[...].astype(F32) + branch_ref[...].astype(F32)
    f_ref[...] = (resid * inv_rms(resid) * gain_ref[1:2, :]).astype(BF16)


def ffn_spans(dp, col, half, chunk, n_dp):
    return [pl.ds(pl.multiple_of(col * half, half), half)] + [
        pl.ds(pl.multiple_of((1 - col) * half + (dp ^ a) * chunk, chunk), chunk)
        for a in range(n_dp)
    ]


def ffn_body(n_dp, tiles, ids, f_ref, c_ref, *refs):
    count = n_dp + 1
    gates, ups, downs = refs[:count], refs[count : 2 * count], refs[2 * count : 3 * count]
    h_ref, dg_ref, du_ref, out_ref, sd_ref, sg_ref, su_ref = refs[3 * count : 3 * count + 7]
    acc, h_scr, dg_scr, du_scr, into_scr, down_scr = refs[3 * count + 7 :]
    step = pl.program_id(0)
    half, tile = gates[0].shape
    col = ids[2]
    spans = ffn_spans(ids[0], col, half, gates[1].shape[0], n_dp)

    @pl.when(step == 0)
    def _():
        acc[...] = jnp.zeros_like(acc)

    @pl.when(step < tiles)
    def _():
        for span, g, u, d in zip(spans, gates, ups, downs):
            into_scr[span, :tile] = g[...]
            into_scr[span, tile:] = u[...]
            down_scr[:, span] = d[...]
        f = f_ref[...]
        gate, up = dot(f, into_scr[:, :tile]), dot(f, into_scr[:, tile:])
        d_hid = dot_nt(c_ref[...], down_scr[...])
        root = math.sqrt(2.0 / math.pi)
        square = gate * gate
        tanh = jnp.tanh(gate * (root + (root * 0.044715) * square))
        bell = 0.5 + 0.5 * tanh
        slope = bell + (0.5 * gate) * (1.0 - tanh * tanh) * (root + (3 * root * 0.044715) * square)
        act = gate * bell
        hidden = (act * up).astype(BF16)
        d_gate = (d_hid * up * slope).astype(BF16)
        d_up = (d_hid * act).astype(BF16)
        units = pl.ds(pl.multiple_of(step * tile, tile), tile)
        for out, scr, value in (
            (h_ref, h_scr, hidden),
            (dg_ref, dg_scr, d_gate),
            (du_ref, du_scr, d_up),
        ):
            out[...] = value
            scr[:, units] = value
        acc[...] += dot_nt(jnp.concatenate([d_gate, d_up], axis=1), into_scr[...])

    @pl.when(step == tiles - 1)
    def _():
        out_ref[...] = acc[...].astype(BF16)

    @pl.when(step >= tiles)
    def _():
        side = (1 - (step - tiles)) ^ col
        core = (ids[0] & 1) ^ 1
        rows, units = sg_ref.shape[1], sd_ref.shape[1]
        left = f_ref[:, pl.ds(pl.multiple_of((side * 2 + core) * rows, rows), rows)].T
        for out, scr in ((sg_ref, dg_scr), (su_ref, du_scr)):
            for j in range(tiles):
                cols = slice(j * tile, (j + 1) * tile)
                out[0, :, cols] = dot(left, scr[:, cols]).astype(BF16)
        cot = c_ref[:, pl.ds(pl.multiple_of(side * half, half), half)]
        cut = units // 3
        for k in range(3):
            place = pl.multiple_of(core * units + k * cut, cut)
            left = h_scr[:, pl.ds(place, cut)].T
            sd_ref[0, k * cut : (k + 1) * cut, :] = dot(left, cot).astype(BF16)


def down_body(n_dp, ids, h_ref, *refs):
    downs = refs[: n_dp + 1]
    out_ref = refs[n_dp + 1]
    spans = ffn_spans(ids[0], ids[2], downs[0].shape[1], downs[1].shape[1], n_dp)
    for span, d in zip(spans, downs):
        out_ref[:, span] = dot(h_ref[...], d[...]).astype(BF16)


def grad_in_body(tile, ids, f_ref, d_ref, got_ref, theirs_ref, mine_ref):
    rows = mine_ref.shape[0]
    for i, out in enumerate((theirs_ref, mine_ref)):
        place = (((1 - i) ^ ids[2]) * 2 + (ids[0] & 1)) * rows
        left = f_ref[:, pl.ds(pl.multiple_of(place, rows), rows)].T
        for j in range(d_ref.shape[1] // tile):
            cols = slice(j * tile, (j + 1) * tile)
            res = dot(left, d_ref[:, cols]) + got_ref[i, :, cols].astype(F32)
            out[:, cols] = res.astype(BF16)


def grad_in_y_body(tile, ids, f_ref, d_ref, got_ref, *outs):
    rows = outs[0].shape[0]
    y = ids[0] // 2
    for h in range(2):
        for i in range(2):
            cut = ((1 - h) ^ y) * rows
            place = (((1 - i) ^ ids[2]) * 2 + (ids[0] & 1)) * 2 * rows + cut
            left = f_ref[:, pl.ds(pl.multiple_of(place, rows), rows)].T
            got = got_ref.at[i, pl.ds(pl.multiple_of(cut, rows), rows)]
            for j in range(d_ref.shape[1] // tile):
                cols = slice(j * tile, (j + 1) * tile)
                res = dot(left, d_ref[:, cols]) + got[:, cols].astype(F32)
                outs[h * 2 + i][:, cols] = res.astype(BF16)


def grad_down_body(tile, ids, h_ref, c_ref, got_ref, first_ref, second_ref, mine_ref):
    units, half = mine_ref.shape
    cut = half // 2
    for k in range(units // tile):
        place = pl.multiple_of((ids[0] & 1) * units + k * tile, tile)
        left = h_ref[:, pl.ds(place, tile)].T
        rows = slice(k * tile, (k + 1) * tile)
        for i in range(2):
            cols = pl.ds(pl.multiple_of(((1 - i) ^ ids[2]) * half, half), half)
            res = (dot(left, c_ref[:, cols]) + got_ref[i, rows, :].astype(F32)).astype(BF16)
            if i == 0:
                first_ref[rows, :] = res[:, :cut]
                second_ref[rows, :] = res[:, cut:]
            else:
                mine_ref[rows, :] = res


def own_body(ids, d_ref, x_ref, branch_ref, cot_ref, gain_ref, dres_ref, low_ref, part_ref):
    resid = x_ref[...].astype(F32) + branch_ref[...].astype(F32)
    r2 = inv_rms(resid)
    n2 = resid * r2
    d = d_ref[...].astype(F32)
    u = d * gain_ref[1:2, :]
    d_resid = cot_ref[...].astype(F32) + r2 * (u - n2 * jnp.mean(u * n2, axis=-1, keepdims=True))
    dres_ref[...] = d_resid
    low_ref[...] = d_resid.astype(BF16)
    part_ref[...] = jnp.broadcast_to(jnp.sum(d * n2, axis=0, keepdims=True), part_ref.shape)


def attend_back_body(n_row, n_col, heads, ids, *refs):
    q_ref, own_ref, oth_ref, lo_ref, hi_ref, l_ref, cos_ref, sin_ref = refs[:8]
    refs = refs[8:]
    db_ref, w_ref, dq_ref, out_ref, kv_own, kv_oth, dm_ref = refs
    dm_ref[...] = dot_nt(db_ref[...], w_ref[...]).astype(BF16)
    col = ids[2]
    n = q_ref.shape[0] // n_row
    kv_own[...] = jnp.zeros_like(kv_own)
    kv_oth[...] = jnp.zeros_like(kv_oth)
    for r in range(n_row):
        rows = slice(r * n, (r + 1) * n)
        count = (r + 1) * n
        q = stack_heads(q_ref[rows, :], heads)
        dm = stack_heads(dm_ref[rows, :], heads)
        lo = jnp.concatenate([lo_ref[rows, :]] * heads, axis=0)
        hi = jnp.concatenate([hi_ref[rows, :]] * heads, axis=0)
        log_total = jnp.concatenate([l_ref[rows, h : h + 1] for h in range(heads)], axis=0)
        oks = key_masks(lo, hi, count, n, n_col, col)
        probs, d_probs = [], []
        for ok, kv_ref in zip(oks, (own_ref, oth_ref)):
            scores = dot_nt(q, kv_ref[:count, :HEAD])
            probs.append(jnp.where(ok, jnp.exp(jnp.where(ok, scores - log_total, NEG_FILL)), 0.0))
            d_probs.append(dot_nt(dm, kv_ref[:count, HEAD:]))
        mean = jnp.sum(probs[0] * d_probs[0], axis=-1, keepdims=True) + jnp.sum(
            probs[1] * d_probs[1], axis=-1, keepdims=True
        )
        dq = None
        for p, dpr, kv_ref, acc in zip(probs, d_probs, (own_ref, oth_ref), (kv_own, kv_oth)):
            ds = (p * (dpr - mean)).astype(BF16)
            part = dot(ds, kv_ref[:count, :HEAD])
            dq = part if dq is None else dq + part
            acc[:count, :HEAD] += dot_tn(ds, q)
            acc[:count, HEAD:] += dot_tn(p.astype(BF16), dm)
        cos_part, sin_part = cos_ref[rows, :], sin_ref[rows, :]
        for h in range(heads):
            piece = turn(dq[h * n : (h + 1) * n], cos_part, -sin_part) * SCALE
            dq_ref[rows, h * HEAD : (h + 1) * HEAD] = piece.astype(BF16)
    for r in range(n_row):
        rows = slice(r * n, (r + 1) * n)
        out_ref[r * n_col + col] = kv_own[rows, :].astype(BF16)
        out_ref[r * n_col + 1 - col] = kv_oth[rows, :].astype(BF16)


def keyval_body(ids, cos_ref, sin_ref, pieces_ref, out_ref):
    total = jnp.sum(pieces_ref[...].astype(F32), axis=0)
    out_ref[:, :HEAD] = turn(total[:, :HEAD], cos_ref[...], -sin_ref[...]).astype(BF16)
    out_ref[:, HEAD:] = total[:, HEAD:].astype(BF16)


def deal_rows(n_row, n_col, shard, ids, res, line_of, send_ref, keep_ref):
    step = pl.program_id(0)
    other = (step & 1) == 0
    for r in range(n_row):
        for c in range(n_col):
            k = r * n_col + c
            block = res[k * shard : (k + 1) * shard]
            if line_of is not None:
                line = lax.broadcasted_iota(jnp.int32, (16, res.shape[1]), 0)
                wide = jnp.broadcast_to(line_of(k), (16, res.shape[1]))
                pad = jnp.where(line == 0, wide, 0.0).astype(BF16)
                block = jnp.concatenate([block, pad], axis=0)
            tall = block.shape[0]
            spot = (step // 2) * n_col + c

            @pl.when(other)
            def _():
                send_ref[spot, r * tall : (r + 1) * tall, :] = block

            @pl.when(jnp.logical_not(other))
            def _():
                keep_ref[spot, r * tall : (r + 1) * tall, :] = block


def project_out_body(n_dp, n_col, ids, mixed_ref, db_ref, send_ref, keep_ref, scr):
    scr[...] = mixed_ref[...].T
    shard = send_ref.shape[1]
    rows = n_col * shard
    for y in range(n_dp // 2):
        for flip, out in ((1, send_ref), (0, keep_ref)):
            place = pl.multiple_of((y * 2 + ((ids[0] & 1) ^ flip)) * rows, rows)
            res = dot(scr[pl.ds(place, rows), :], db_ref[...]).astype(BF16)
            for c in range(n_col):
                out[y * n_col + c] = res[c * shard : (c + 1) * shard]


def project_in_body(n_row, n_col, shard, ids, left_ref, dq_ref, dkv_ref, gain_ref, *refs):
    send_ref, keep_ref, scr = refs
    scr[...] = left_ref[...].T
    n = dkv_ref.shape[0]
    own = scr[:, pl.ds(pl.multiple_of(ids[1] * n, n), n)]
    res = jnp.concatenate(
        [dot(scr[...], dq_ref[...]).astype(BF16), dot(own, dkv_ref[...]).astype(BF16)], axis=1
    )
    deal_rows(
        n_row, n_col, shard, ids, res, lambda k: gain_ref[k : k + 1, :], send_ref, keep_ref
    )


def attn_grad_body(ids, d_ref, w_ref, out_ref):
    out_ref[...] = dot_nt(d_ref[...], w_ref[:, : d_ref.shape[1]]).astype(BF16)


def token_body(ids, d_ref, dkv_ref, wkv_ref, x_ref, gain_ref, dres_ref, out_ref):
    d = d_ref[...].astype(F32) + dot_nt(dkv_ref[...], wkv_ref[:, wkv_ref.shape[1] - 2 * HEAD :])
    x = x_ref[...].astype(F32)
    r1 = inv_rms(x)
    n1 = x * r1
    u = d * gain_ref[0:1, :]
    out = dres_ref[...] + r1 * (u - n1 * jnp.mean(u * n1, axis=-1, keepdims=True))
    out_ref[...] = out.astype(BF16)


def last_body(n_row, hcols, ids, pieces_ref, wq_ref, wkv_ref, gain_ref, *refs):
    gq_ref, gkv_ref, ga_ref, gf_ref = refs
    shard = gq_ref.shape[0]
    gkv = jnp.sum(pieces_ref[:, :shard, hcols:].astype(F32), axis=0)
    gkv_ref[...] = gkv
    gf_ref[...] = jnp.sum(pieces_ref[:, shard:, :].astype(F32), axis=0)[:8]
    total = jnp.sum(gkv * wkv_ref[...].astype(F32), axis=-1, keepdims=True)
    for r in range(n_row):
        cols = slice(r * hcols, (r + 1) * hcols)
        part = pieces_ref[r, :shard, :hcols].astype(F32)
        gq_ref[:, cols] = part
        total = total + jnp.sum(part * wq_ref[:, cols].astype(F32), axis=-1, keepdims=True)
    ga_ref[...] = total / gain_ref[...]


def join_body(ids, mine_ref, rest_ref, out_ref):
    rows = out_ref.shape[0]
    count = mine_ref.shape[0] // rows
    step = pl.program_id(0)
    place = pl.ds(pl.multiple_of((step % count) * rows, rows), rows)
    mine = (ids[0] & 1) == step // count

    @pl.when(mine)
    def _():
        out_ref[...] = mine_ref[place, :].astype(F32)

    @pl.when(jnp.logical_not(mine))
    def _():
        out_ref[...] = rest_ref[place, :].astype(F32)


def join_four_body(ids, own_ref, other_ref, own_rest_ref, other_rest_ref, out_ref):
    step = pl.program_id(0)
    core, y = ids[0] & 1, ids[0] // 2
    for flip, parts in ((0, (own_ref, other_ref)), (1, (own_rest_ref, other_rest_ref))):
        for k, part in enumerate(parts):

            @pl.when(step == (core ^ flip) * 2 + (y ^ k))
            def _():
                out_ref[...] = part[...].astype(F32)


def layout(length_row, order_row, where_at):
    slot_ids = jnp.arange(length_row.shape[0], dtype=jnp.int32)
    placed = jnp.sum(
        jnp.where(order_row[:, None] == slot_ids[None, :], length_row[None, :], 0),
        axis=1,
        dtype=jnp.int32,
    )
    before = jnp.where(slot_ids[None, :] < slot_ids[:, None], placed[None, :], 0)
    starts = jnp.sum(before, axis=1, dtype=jnp.int32)
    ends = starts + placed
    within = (where_at[:, None] >= starts[None, :]) & (where_at[:, None] < ends[None, :])
    begin = jnp.sum(jnp.where(within, starts[None, :], 0), axis=1, dtype=jnp.int32)
    return jnp.where(where_at < jnp.sum(placed), where_at - begin, 0)


def add_body(ids, left_ref, right_ref, out_ref):
    out_ref[...] = (left_ref[...].astype(F32) + right_ref[...].astype(F32)).astype(BF16)


def three_body(ids, a_ref, b_ref, c_ref, out_ref):
    total = a_ref[...].astype(F32) + b_ref[...].astype(F32) + c_ref[...].astype(F32)
    out_ref[...] = total.astype(BF16)


def beside_body(ids, left_ref, first_ref, second_ref, out_ref):
    cut = first_ref.shape[1]
    for k, part in enumerate((first_ref, second_ref)):
        cols = slice(k * cut, (k + 1) * cut)
        total = left_ref[:, cols].astype(F32) + part[...].astype(F32)
        out_ref[:, cols] = total.astype(BF16)


def tile_of(size, wanted):
    while size % wanted:
        wanted //= 2
    return wanted


def shards(
    tokens,
    cotangent,
    w_query,
    w_keyval,
    w_out,
    norm_attn,
    norm_ffn,
    w_gate,
    w_up,
    w_down,
    lengths,
    placement,
):
    n_y, n_row, n_col = lax.axis_size("y"), lax.axis_size("row"), lax.axis_size("col")
    n_dp = 2 * n_y
    dp, row, col = lax.axis_index(DP), lax.axis_index("row"), lax.axis_index("col")
    ids = jnp.stack([dp, row, col]).astype(jnp.int32)
    n, width = tokens.shape
    half = width // n_col
    rows_all = n_row * n
    heads = HEADS // n_row
    hcols = heads * HEAD
    part = width // n_row
    shard = w_query.shape[0]
    ffn = w_gate.shape[1]
    chunk = half // n_dp
    used = hcols + 2 * HEAD
    tall = shard + 16

    def add_low(left, right):
        return run(add_body, ids, [left, right], [None, None], [sds(left.shape)], [None])[0]

    zeros = jnp.zeros((1, used - shard), BF16)
    pack = run(
        functools.partial(pack_body, n_row),
        ids,
        [w_query, w_keyval]
        + [jnp.concatenate([g[None, :], zeros], axis=1) for g in (norm_attn, norm_ffn)],
        [None] * 4,
        [sds((n_row, tall, used))],
        [None],
    )[0]
    packed = deal(pack, "row").reshape(1, n_row * tall, used)
    x_low = lax.all_gather(tokens, "row", axis=0, tiled=True)
    wo_turned = transpose_devices(after(w_out, packed))[None]
    around = n_y * n_col
    pack_own = deal(jnp.broadcast_to(packed, (around,) + packed.shape[1:]), ("y", "col"))
    pack_oth = swap_core(pack_own)
    cot = lax.all_gather(after(cotangent, pack_own), "row", axis=0, tiled=True)

    where_at = (
        (jnp.arange(n_row, dtype=jnp.int32) * (n_col * n))[:, None]
        + jnp.arange(n, dtype=jnp.int32)
        + col * n
    ).reshape(-1)
    offset = layout(lengths[0], placement[0], where_at)
    low_at, high_at = (where_at - offset)[:, None], where_at[:, None]
    frequency = ROPE_BASE ** (-2.0 * jnp.arange(HEAD // 2, dtype=jnp.int32).astype(F32) / HEAD)
    angle = offset.astype(F32)[:, None] * frequency[None, :]
    cos_part, sin_part = jnp.cos(angle), jnp.sin(angle)
    cos_all = jnp.concatenate([cos_part, cos_part], axis=1)
    sin_all = jnp.concatenate([-sin_part, sin_part], axis=1)

    attn_in, kv_own, query, w_qkv, gains = run(
        functools.partial(front_body, n_row, n_col, hcols, shard),
        ids,
        [x_low, pack_own, pack_oth, cos_all, sin_all],
        [None, None, None, None, None],
        [
            sds((rows_all, width)),
            sds((rows_all, 2 * HEAD)),
            sds((rows_all, hcols)),
            sds((width, used)),
            sds((8, width), F32),
        ],
        [None, None, None, None, None],
        scratch=[pltpu.VMEM((width // shard, HEAD), F32)] * 2,
    )
    kv_oth = swap_col(kv_own)
    wo_own = deal(
        jnp.broadcast_to(after(wo_turned, kv_own), (around,) + wo_turned.shape[1:]),
        ("y", "col"),
    )
    mixed, log_total = run(
        functools.partial(attend_body, n_row, n_col, heads),
        ids,
        [query, kv_own, kv_oth, low_at, high_at],
        [None] * 5,
        [sds((rows_all, hcols)), sds((rows_all, HEAD), F32)],
        [None] * 2,
    )
    wo_oth = swap_core(after(wo_own, mixed))
    gate_cut, up_cut, down_cut = run(
        cut_body,
        ids,
        [w_gate, w_up, after(w_down, mixed)],
        [pl.BlockSpec((chunk, ffn), lambda i, ids: (ids[0], 0))] * 2
        + [pl.BlockSpec((ffn, chunk), lambda i, ids: (0, ids[0]))],
        [sds((chunk, ffn))] * 2 + [sds((ffn, chunk))],
        [None] * 3,
    )
    gate_got = swap_col(gate_cut)
    up_got = swap_col(after(up_cut, gate_got))
    down_got = swap_col(after(down_cut, up_got))
    gate_y = [gate_got] + [swap_y(gate_got, k) for k in range(1, n_y)]
    up_y = [up_got] + [swap_y(up_got, k) for k in range(1, n_y)]
    down_y = [down_got] + [swap_y(down_got, k) for k in range(1, n_y)]
    part_branch, w_rows = run(
        functools.partial(branch_body, n_col),
        ids,
        [mixed, wo_own, wo_oth],
        [None, None, None],
        [sds((rows_all, width)), sds((hcols, width))],
        [None] * 2,
    )
    branch = lax.psum_scatter(after(part_branch, cot), "row", scatter_dimension=0, tiled=True)
    ffn_own_in = run(
        norm_body,
        ids,
        [tokens, after(branch, up_got, *gate_y), gains],
        [None] * 3,
        [sds((n, width))],
        [None],
    )[0]
    ffn_in = lax.all_gather(ffn_own_in, "row", axis=0, tiled=True)

    def with_core(own, around_y):
        return [own] + [x for g in around_y for x in (g, swap_core(after(g, part_branch)))]

    gates, ups, downs = (
        with_core(w_gate, gate_y),
        with_core(w_up, up_y),
        with_core(w_down, down_y),
    )

    tile = tile_of(ffn, 512)
    tiles = ffn // tile
    quarter = half // 2

    def at(j):
        return jnp.minimum(j, tiles - 1)

    def once(array):
        zeros = (0,) * len(array.shape)
        return pl.BlockSpec(array.shape, lambda *_: zeros, pipeline_mode=pl.Buffered(1))

    into = [pl.BlockSpec((half, tile), lambda j, ids: (0, at(j)))] + [
        pl.BlockSpec((chunk, tile), lambda j, ids: (0, at(j)))
    ] * n_dp
    late = lambda j, ids: (jnp.maximum(j - tiles, 0), 0, 0)
    hidden, d_gate, d_up, d_ffn, sent_down, sent_gate, sent_up = run(
        functools.partial(ffn_body, n_dp, tiles),
        ids,
        [ffn_in, cot] + gates + ups + downs,
        [once(ffn_in), once(cot)]
        + into * 2
        + [pl.BlockSpec((tile, half), lambda j, ids: (at(j), 0))]
        + [pl.BlockSpec((tile, chunk), lambda j, ids: (at(j), 0))] * n_dp,
        [sds((rows_all, ffn))] * 3
        + [sds((rows_all, width)), sds((2, ffn // 2, half))]
        + [sds((2, quarter, ffn))] * 2,
        [pl.BlockSpec((rows_all, tile), lambda j, ids: (0, at(j)))] * 3
        + [None, pl.BlockSpec((1, ffn // 2, half), late)]
        + [pl.BlockSpec((1, quarter, ffn), late)] * 2,
        grid=(tiles + 2,),
        scratch=[pltpu.VMEM((rows_all, width), F32)]
        + [pltpu.VMEM((rows_all, ffn), BF16)] * 3
        + [pltpu.VMEM((width, 2 * tile), BF16), pltpu.VMEM((tile, width), BF16)],
        limit=60,
    )
    d_own = lax.psum_scatter(d_ffn, "row", scatter_dimension=0, tiled=True)

    ft = tile_of(ffn, 512)
    rt = tile_of(ffn // 2, 256)

    def grad_in(right, got, *gate_on):
        body = functools.partial(grad_in_body, ft)
        args = [after(ffn_in, *gate_on), right, got]
        return run(body, ids, args, [None] * 3, [sds((quarter, ffn))] * 2, [None] * 2)

    def grad_in_y(right, got, *gate_on):
        return run(
            functools.partial(grad_in_y_body, ft),
            ids,
            [after(ffn_in, *gate_on), right, got],
            [None, None, None],
            [sds((quarter // 2, ffn))] * 4,
            [None] * 4,
        )

    def grad_down_part(got, *gate_on):
        body = functools.partial(grad_down_body, rt)
        args = [after(hidden, *gate_on), cot, got]
        outs = [sds((ffn // 2, half // 2))] * 2 + [sds((ffn // 2, half))]
        return run(body, ids, args, [None] * 3, outs, [None] * 3)

    got_down = swap_core(sent_down)
    got_gate = swap_core(sent_gate)
    got_up = swap_core(sent_up)
    theirs_first, theirs_second, mine_down = grad_down_part(got_down, d_ffn)
    col_first = swap_col(theirs_first)
    if n_y == 2:
        send_theirs, send_mine, keep_theirs, keep_mine = grad_in_y(d_gate, got_gate, theirs_first)
        y_theirs = swap_y(send_theirs, 1)
        early = [col_first, y_theirs]
    else:
        theirs_gate, keep_mine = grad_in(d_gate, got_gate, theirs_first)
        early = [col_first]
    ffn_out = run(
        functools.partial(down_body, n_dp),
        ids,
        [after(hidden, keep_mine)] + downs,
        [None] * (2 + n_dp),
        [sds((rows_all, width))],
        [None],
    )[0]

    d_resid, d_low, gain_part = run(
        own_body,
        ids,
        [after(d_own, ffn_out), tokens, branch, cotangent, gains],
        [None] * 5,
        [sds((n, width), F32), sds((n, width)), sds((8, width), F32)],
        [None] * 3,
    )
    d_branch = lax.all_gather(after(d_low, *early), "row", axis=0, tiled=True)
    ffn_own = lax.psum_scatter(after(ffn_out, d_low, *early), "row", scatter_dimension=0, tiled=True)

    def y_total(value, *others):
        total = value
        step = 1
        while step < n_y:
            total = add_low(total, after(swap_y(total, step), *others))
            step *= 2
        return total

    def three(a, b, c):
        return run(three_body, ids, [a, b, c], [None] * 3, [sds(a.shape)], [None])[0]

    col_second = swap_col(after(theirs_second, col_first, d_low))
    if n_y == 2:
        y_mine = swap_y(after(send_mine, y_theirs, d_low), 1)
        theirs_gate = add_low(keep_theirs, after(y_theirs, d_low))
    col_gate = swap_col(theirs_gate)
    theirs_up, mine_up = grad_in(d_up, got_up, d_low, theirs_gate)
    sum_down = run(
        beside_body,
        ids,
        [mine_down, col_first, after(col_second, theirs_gate)],
        [None] * 3,
        [sds(mine_down.shape)],
        [None],
    )[0]
    col_up = swap_col(after(theirs_up, col_gate))
    if n_y == 2:
        moved_down = swap_y(sum_down, 1)
        sum_gate = three(keep_mine, y_mine, col_gate)
        full_gate = swap_y(sum_gate, 1)
    else:
        moved_down = sum_down
        sum_gate = add_low(keep_mine, col_gate)
        full_gate = y_total(sum_gate)

    d_query, d_kv_parts = run(
        functools.partial(attend_back_body, n_row, n_col, heads),
        ids,
        [query, kv_own, kv_oth, low_at, high_at, log_total, cos_all, sin_all]
        + [after(d_branch, sum_gate, theirs_up, sum_down), w_rows],
        [None] * 10,
        [sds((rows_all, hcols)), sds((n_row * n_col, n, 2 * HEAD))],
        [None] * 2,
        scratch=[pltpu.VMEM((rows_all, 2 * HEAD), F32)] * 2
        + [pltpu.VMEM((rows_all, hcols), BF16)],
    )
    d_kv_parts = deal(d_kv_parts, ("row", "col"))
    d_attn = run(
        attn_grad_body, ids, [after(d_query, moved_down, col_up, full_gate), w_qkv], [None] * 2, [sds((rows_all, width))], [None]
    )[0]
    d_attn_own = lax.psum_scatter(d_attn, "row", scatter_dimension=0, tiled=True)

    result = (tokens.astype(F32) + branch.astype(F32) + ffn_own.astype(F32)).astype(BF16)
    mine = lax.dynamic_slice_in_dim(result, col * half, half, 1)
    moved = swap_col(lax.dynamic_slice_in_dim(result, (1 - col) * half, half, 1))
    result = jnp.where(
        col == 0, jnp.concatenate([mine, moved], axis=0), jnp.concatenate([moved, mine], axis=0)
    )

    by_dp = width // n_dp

    def block_of(j, ids):
        return (j // 2) * 2 + ((ids[0] & 1) ^ ((j & 1) ^ 1))

    lines = n_row * n_col
    gain_lines = jnp.pad(
        gain_part[0].reshape(n_dp * lines, shard), ((0, 0), (0, used - shard))
    )
    own_cos = lax.dynamic_slice_in_dim(cos_all, row * n, n, 0)
    own_sin = lax.dynamic_slice_in_dim(sin_all, row * n, n, 0)
    d_kv = run(
        keyval_body,
        ids,
        [own_cos, own_sin, after(d_kv_parts, d_attn)],
        [None, None, None],
        [sds((n, 2 * HEAD))],
        [None],
    )[0]
    send_q, keep_q = run(
        functools.partial(project_in_body, n_row, n_col, shard),
        ids,
        [attn_in, d_query, d_kv, gain_lines],
        [
            pl.BlockSpec((rows_all, by_dp), lambda j, ids: (0, block_of(j, ids))),
            None,
            None,
            pl.BlockSpec((lines, used), lambda j, ids: (block_of(j, ids), 0)),
        ],
        [sds((around, n_row * tall, used))] * 2,
        [None] * 2,
        grid=(n_dp,),
        scratch=[pltpu.VMEM((by_dp, rows_all), BF16)],
    )
    got_q = swap_core(send_q)
    if n_y == 2:
        full_down = add_low(sum_down, after(moved_down, send_q))
        sum_up = add_low(mine_up, after(col_up, full_down))
        moved_up = swap_y(sum_up, 1)
    else:
        full_down = y_total(sum_down)
        sum_up = moved_up = add_low(mine_up, after(col_up, full_down, full_gate))
    send_o, keep_o = run(
        functools.partial(project_out_body, n_dp, n_col),
        ids,
        [mixed, after(d_branch, sum_up)],
        [None] * 2,
        [sds((around, shard, width))] * 2,
        [None] * 2,
        scratch=[pltpu.VMEM((hcols, rows_all), BF16)],
    )
    o_total = keep_o.astype(F32) + swap_core(send_o).astype(F32)
    o_total = o_total.astype(BF16)

    def parts_sum(total, *others):
        dealt = after(deal(total, ("y", "col")), *others)
        return jnp.sum(dealt.astype(F32), axis=0).astype(BF16)

    q_total = (keep_q.astype(F32) + after(got_q, full_down).astype(F32)).astype(BF16)
    def joined(mine, shape):
        return run(
            join_body,
            ids,
            [mine, swap_core(mine)],
            [None] * 2,
            [sds(shape, F32)],
            [pl.BlockSpec((shape[0] // 4, shape[1]), lambda b, ids: (b, 0))],
            grid=(4,),
        )[0]

    grad_down = joined(after(full_down, got_q), (ffn, half))
    def join_four(parts):
        return run(
            join_four_body,
            ids,
            parts + [swap_core(p) for p in parts],
            [None] * 4,
            [sds((half, ffn), F32)],
            [pl.BlockSpec((half // 4, ffn), lambda b, ids: (b, 0))],
            grid=(4,),
        )[0]

    if n_y == 2:
        grad_gate = join_four([sum_gate, after(full_gate, grad_down)])
    else:
        grad_gate = joined(full_gate, (half, ffn))

    grad_tokens = run(
        token_body,
        ids,
        [d_attn_own, d_kv, w_qkv, tokens, gains, d_resid],
        [None] * 6,
        [sds((n, width))],
        [None],
    )[0]

    q_sum = parts_sum(q_total, grad_down, grad_gate, grad_tokens, result, moved_up)
    if n_y == 2:
        full_up = add_low(sum_up, after(moved_up, q_sum))
    else:
        full_up = y_total(sum_up, q_sum)
    q_pieces = deal(q_sum.reshape(n_row, tall, used), "row")
    o_sum = parts_sum(after(o_total, q_sum))
    grad_out = transpose_devices(after(o_sum, q_pieces)).astype(F32)
    grad_up = joined(full_up, (half, ffn))
    grad_query, grad_keyval, gain_a, gain_f = run(
        functools.partial(last_body, n_row, hcols),
        ids,
        [after(q_pieces, grad_up), w_query, w_keyval, norm_attn.astype(F32)[:, None]],
        [None, None, None, None],
        [
            sds((shard, width), F32),
            sds((shard, 2 * HEAD), F32),
            sds((shard, 1), F32),
            sds((8, used), F32),
        ],
        [None] * 4,
    )
    return (
        result,
        grad_tokens,
        grad_query,
        grad_keyval,
        grad_out,
        gain_a[:, 0],
        gain_f[0, :shard],
        grad_gate,
        grad_up,
        grad_down,
    )


def solution(mesh):
    n_dp, n_row, n_col = (mesh.shape[a] for a in ("dp", "row", "col"))
    fine = jax.sharding.Mesh(mesh.devices.reshape(n_dp // 2, 2, n_row, n_col), EVERY)
    rows = P(EVERY, None)
    in_specs = (
        rows,
        rows,
        rows,
        rows,
        rows,
        P(EVERY),
        P(EVERY),
        P("col", "row"),
        P("col", "row"),
        P("row", "col"),
        P(DP, None),
        P(DP, None),
    )
    out_specs = (
        P(DP + ("row",), "col"),
        rows,
        rows,
        rows,
        rows,
        P(EVERY),
        P(EVERY),
        P("col", "row"),
        P("col", "row"),
        P("row", "col"),
    )
    return jax.shard_map(shards, mesh=fine, in_specs=in_specs, out_specs=out_specs, check_vma=False)
```

```python
import functools
import math

import jax
import jax.numpy as jnp
from jax import lax
from jax.experimental import pallas as pl
from jax.experimental.pallas import tpu as pltpu
from jax.sharding import PartitionSpec as P

HEADS = 16
HEAD = 128

EPSILON = 1e-06
ROPE_BASE = 10000.0
NEG_FILL = -1e30
SCALE = 1.0 / math.sqrt(HEAD)
DP = ("y", "core")
EVERY = ("y", "core", "row", "col")
F32 = jnp.float32
BF16 = jnp.bfloat16
MIB = 2**20


def swap_core(value):
    return lax.ppermute(value, "core", [(0, 1), (1, 0)])


def swap_y(value, k):
    return lax.ppermute(value, "y", [(i, i ^ k) for i in range(lax.axis_size("y"))])


def swap_col(value):
    return lax.ppermute(value, "col", [(0, 1), (1, 0)])


def deal(value, axes):
    return lax.all_to_all(value, axes, split_axis=0, concat_axis=0, tiled=True)


def transpose_devices(value):
    n_dp, n_row, n_col = 2 * lax.axis_size("y"), lax.axis_size("row"), lax.axis_size("col")
    pairs = [
        ((d * n_row + r) * n_col + c, (r * n_row + d) * n_col + c)
        for d in range(n_dp)
        for r in range(n_row)
        for c in range(n_col)
    ]
    return lax.ppermute(value, EVERY, pairs)


def after(value, *others):
    return lax.optimization_barrier((value,) + others)[0]


def dot(left, right):
    return jnp.dot(left, right, preferred_element_type=F32)


def dot_tn(left, right):
    return lax.dot_general(left, right, (((0,), (0,)), ((), ())), preferred_element_type=F32)


def dot_nt(left, right):
    return lax.dot_general(left, right, (((1,), (1,)), ((), ())), preferred_element_type=F32)


def inv_rms(values):
    return lax.rsqrt(jnp.mean(values * values, axis=-1, keepdims=True) + EPSILON)


def run(body, ids, args, in_specs, outs, out_specs, grid=(1,), scratch=(), limit=56):
    def place(spec, array):
        if spec is None:
            zeros = (0,) * len(array.shape)
            return pl.BlockSpec(array.shape, lambda *_: zeros)
        return spec

    in_specs = [place(s, a) for s, a in zip(in_specs, args)]
    out_specs = [place(s, a) for s, a in zip(out_specs, outs)]
    return pl.pallas_call(
        body,
        grid_spec=pltpu.PrefetchScalarGridSpec(
            num_scalar_prefetch=1,
            grid=grid,
            in_specs=in_specs,
            out_specs=out_specs,
            scratch_shapes=list(scratch),
        ),
        out_shape=outs,
        compiler_params=pltpu.CompilerParams(
            vmem_limit_bytes=limit * MIB, dimension_semantics=("arbitrary",) * len(grid)
        ),
        cost_estimate=pl.CostEstimate(flops=0, bytes_accessed=10**5, transcendentals=0),
    )(ids, *args)


def sds(shape, dtype=BF16):
    return jax.ShapeDtypeStruct(shape, dtype)


def turn(values, cos_part, sin_part):
    return values * cos_part + pltpu.roll(values, HEAD // 2, 1) * sin_part


def cut_body(ids, g_ref, u_ref, d_ref, g_out, u_out, d_out):
    g_out[...] = g_ref[...]
    u_out[...] = u_ref[...]
    d_out[...] = d_ref[...]


def pack_body(n_row, ids, wq_ref, wkv_ref, ga_ref, gf_ref, out_ref):
    shard, kv = wkv_ref.shape
    hcols = wq_ref.shape[1] // n_row
    used = hcols + kv
    for r in range(n_row):
        out_ref[r, :shard, :hcols] = wq_ref[:, r * hcols : (r + 1) * hcols]
        out_ref[r, :shard, hcols:] = wkv_ref[...]
        line = lax.broadcasted_iota(jnp.int32, (16, used), 0)
        ga = jnp.broadcast_to(ga_ref[...].astype(F32), (16, used))
        gf = jnp.broadcast_to(gf_ref[...].astype(F32), (16, used))
        tail = jnp.where(line == 0, ga, jnp.where(line == 1, gf, 0.0))
        out_ref[r, shard:, :] = tail.astype(BF16)


def front_body(n_row, n_col, hcols, shard, ids, x_ref, own_ref, oth_ref, cos_ref, sin_ref, *refs):
    a_ref, kv_ref, q_ref, w_ref, gain_ref, g0, g1 = refs
    core = ids[0] & 1
    tall = shard + 16
    width = a_ref.shape[1]
    for flip, pack in ((0, own_ref), (1, oth_ref)):
        for p in range(pack.shape[0]):
            y, c = p // n_col, p % n_col
            for z in range(n_row):
                place = ((y * 2 + (core ^ flip)) * n_row + z) * n_col + c
                rows = pl.ds(pl.multiple_of(place * shard, shard), shard)
                w_ref[rows, :] = pack[p, z * tall : z * tall + shard, :]
                tail = pack[p, z * tall + shard : (z + 1) * tall, :HEAD].astype(F32)
                g0[pl.ds(place, 1), :] = tail[0:1]
                g1[pl.ds(place, 1), :] = tail[1:2]
    count = width // shard
    pick = lax.broadcasted_iota(jnp.int32, (HEAD, width), 0)
    feature = lax.broadcasted_iota(jnp.int32, (HEAD, width), 1)
    spread = ((feature & (shard - 1)) == pick).astype(F32)
    home = lax.broadcasted_iota(jnp.int32, (count, width), 0)
    mine = (lax.broadcasted_iota(jnp.int32, (count, width), 1) & ~(shard - 1)) == home * shard
    lines = []
    for g in (g0, g1):
        wide = jnp.dot(g[...], spread, preferred_element_type=F32)
        lines.append(jnp.sum(jnp.where(mine, wide, 0.0), axis=0, keepdims=True))
    gain = lines[0]
    gain_ref[...] = jnp.concatenate(lines * 4, axis=0)
    rows_all = x_ref.shape[0]
    step = 128
    for r in range(rows_all // step):
        rows = slice(r * step, (r + 1) * step)
        x = x_ref[rows, :].astype(F32)
        a_ref[rows, :] = (x * inv_rms(x) * gain).astype(BF16)
    kv = dot(a_ref[...], w_ref[:, hcols:])
    key = turn(kv[:, :HEAD], cos_ref[...], sin_ref[...])
    kv_ref[:, :HEAD] = key.astype(BF16)
    kv_ref[:, HEAD:] = kv[:, HEAD:].astype(BF16)
    raw = dot(a_ref[...], w_ref[:, :hcols])
    for h in range(hcols // HEAD):
        cols = slice(h * HEAD, (h + 1) * HEAD)
        q_ref[:, cols] = (turn(raw[:, cols], cos_ref[...], sin_ref[...]) * SCALE).astype(BF16)


def stack_heads(block, heads):
    return jnp.concatenate([block[:, h * HEAD : (h + 1) * HEAD] for h in range(heads)], axis=0)


def key_masks(lo, hi, count, n, n_col, col):
    j = lax.broadcasted_iota(jnp.int32, (1, count), 1)
    at = j + (j - (j & (n - 1))) * (n_col - 1)
    own, oth = at + col * n, at + (1 - col) * n
    return (own >= lo) & (own <= hi), (oth >= lo) & (oth <= hi)


def attend_body(n_row, n_col, heads, ids, q_ref, own_ref, oth_ref, lo_ref, hi_ref, m_ref, l_ref):
    col = ids[2]
    n = q_ref.shape[0] // n_row
    for r in range(n_row):
        rows = slice(r * n, (r + 1) * n)
        count = (r + 1) * n
        q = stack_heads(q_ref[rows, :], heads)
        lo = jnp.concatenate([lo_ref[rows, :]] * heads, axis=0)
        hi = jnp.concatenate([hi_ref[rows, :]] * heads, axis=0)
        ok_own, ok_oth = key_masks(lo, hi, count, n, n_col, col)
        s_own = jnp.where(ok_own, dot_nt(q, own_ref[:count, :HEAD]), NEG_FILL)
        s_oth = jnp.where(ok_oth, dot_nt(q, oth_ref[:count, :HEAD]), NEG_FILL)
        peak = jnp.maximum(
            jnp.max(s_own, axis=-1, keepdims=True), jnp.max(s_oth, axis=-1, keepdims=True)
        )
        e_own = jnp.where(ok_own, jnp.exp(s_own - peak), 0.0)
        e_oth = jnp.where(ok_oth, jnp.exp(s_oth - peak), 0.0)
        total = jnp.sum(e_own, axis=-1, keepdims=True) + jnp.sum(e_oth, axis=-1, keepdims=True)
        share = 1.0 / total
        mixed = dot((e_own * share).astype(BF16), own_ref[:count, HEAD:]) + dot(
            (e_oth * share).astype(BF16), oth_ref[:count, HEAD:]
        )
        for h in range(heads):
            m_ref[rows, h * HEAD : (h + 1) * HEAD] = mixed[h * n : (h + 1) * n].astype(BF16)
        log_total = peak + jnp.log(total)
        for h in range(heads):
            l_ref[rows, h : h + 1] = log_total[h * n : (h + 1) * n]


def branch_body(n_col, ids, mixed_ref, own_ref, oth_ref, part_ref, w_ref):
    core = ids[0] & 1
    shard = own_ref.shape[1]
    for flip, piece in ((0, own_ref), (1, oth_ref)):
        for p in range(piece.shape[0]):
            place = ((p // n_col) * 2 + (core ^ flip)) * n_col + p % n_col
            rows = pl.ds(pl.multiple_of(place * shard, shard), shard)
            w_ref[rows, :] = piece[p]
    part_ref[...] = dot(mixed_ref[...], w_ref[...]).astype(BF16)


def norm_body(ids, x_ref, branch_ref, gain_ref, f_ref):
    resid = x_ref[...].astype(F32) + branch_ref[...].astype(F32)
    f_ref[...] = (resid * inv_rms(resid) * gain_ref[1:2, :]).astype(BF16)


def ffn_spans(dp, col, half, chunk, n_dp):
    return [pl.ds(pl.multiple_of(col * half, half), half)] + [
        pl.ds(pl.multiple_of((1 - col) * half + (dp ^ a) * chunk, chunk), chunk)
        for a in range(n_dp)
    ]


def ffn_body(n_dp, tiles, ids, f_ref, c_ref, *refs):
    count = n_dp + 1
    gates, ups, downs = refs[:count], refs[count : 2 * count], refs[2 * count : 3 * count]
    h_ref, dg_ref, du_ref, out_ref, sd_ref, sg_ref, su_ref = refs[3 * count : 3 * count + 7]
    acc, h_scr, dg_scr, du_scr, into_scr, down_scr = refs[3 * count + 7 :]
    step = pl.program_id(0)
    half, tile = gates[0].shape
    col = ids[2]
    spans = ffn_spans(ids[0], col, half, gates[1].shape[0], n_dp)

    @pl.when(step == 0)
    def _():
        acc[...] = jnp.zeros_like(acc)

    @pl.when(step < tiles)
    def _():
        for span, g, u, d in zip(spans, gates, ups, downs):
            into_scr[span, :tile] = g[...]
            into_scr[span, tile:] = u[...]
            down_scr[:, span] = d[...]
        f = f_ref[...]
        gate, up = dot(f, into_scr[:, :tile]), dot(f, into_scr[:, tile:])
        d_hid = dot_nt(c_ref[...], down_scr[...])
        root = math.sqrt(2.0 / math.pi)
        square = gate * gate
        tanh = jnp.tanh(gate * (root + (root * 0.044715) * square))
        bell = 0.5 + 0.5 * tanh
        slope = bell + (0.5 * gate) * (1.0 - tanh * tanh) * (root + (3 * root * 0.044715) * square)
        act = gate * bell
        hidden = (act * up).astype(BF16)
        d_gate = (d_hid * up * slope).astype(BF16)
        d_up = (d_hid * act).astype(BF16)
        units = pl.ds(pl.multiple_of(step * tile, tile), tile)
        for out, scr, value in (
            (h_ref, h_scr, hidden),
            (dg_ref, dg_scr, d_gate),
            (du_ref, du_scr, d_up),
        ):
            out[...] = value
            scr[:, units] = value
        acc[...] += dot_nt(jnp.concatenate([d_gate, d_up], axis=1), into_scr[...])

    @pl.when(step == tiles - 1)
    def _():
        out_ref[...] = acc[...].astype(BF16)

    @pl.when(step >= tiles)
    def _():
        side = (1 - (step - tiles)) ^ col
        core = (ids[0] & 1) ^ 1
        rows, units = sg_ref.shape[1], sd_ref.shape[1]
        left = f_ref[:, pl.ds(pl.multiple_of((side * 2 + core) * rows, rows), rows)].T
        for out, scr in ((sg_ref, dg_scr), (su_ref, du_scr)):
            for j in range(tiles):
                cols = slice(j * tile, (j + 1) * tile)
                out[0, :, cols] = dot(left, scr[:, cols]).astype(BF16)
        cot = c_ref[:, pl.ds(pl.multiple_of(side * half, half), half)]
        cut = units // 3
        for k in range(3):
            place = pl.multiple_of(core * units + k * cut, cut)
            left = h_scr[:, pl.ds(place, cut)].T
            sd_ref[0, k * cut : (k + 1) * cut, :] = dot(left, cot).astype(BF16)


def down_body(n_dp, ids, h_ref, *refs):
    downs = refs[: n_dp + 1]
    out_ref = refs[n_dp + 1]
    spans = ffn_spans(ids[0], ids[2], downs[0].shape[1], downs[1].shape[1], n_dp)
    for span, d in zip(spans, downs):
        out_ref[:, span] = dot(h_ref[...], d[...]).astype(BF16)


def grad_in_body(tile, ids, f_ref, d_ref, got_ref, theirs_ref, mine_ref):
    rows = mine_ref.shape[0]
    for i, out in enumerate((theirs_ref, mine_ref)):
        place = (((1 - i) ^ ids[2]) * 2 + (ids[0] & 1)) * rows
        left = f_ref[:, pl.ds(pl.multiple_of(place, rows), rows)].T
        for j in range(d_ref.shape[1] // tile):
            cols = slice(j * tile, (j + 1) * tile)
            res = dot(left, d_ref[:, cols]) + got_ref[i, :, cols].astype(F32)
            out[:, cols] = res.astype(BF16)


def grad_in_y_body(tile, ids, f_ref, d_ref, got_ref, *outs):
    rows = outs[0].shape[0]
    y = ids[0] // 2
    for h in range(2):
        for i in range(2):
            cut = ((1 - h) ^ y) * rows
            place = (((1 - i) ^ ids[2]) * 2 + (ids[0] & 1)) * 2 * rows + cut
            left = f_ref[:, pl.ds(pl.multiple_of(place, rows), rows)].T
            got = got_ref.at[i, pl.ds(pl.multiple_of(cut, rows), rows)]
            for j in range(d_ref.shape[1] // tile):
                cols = slice(j * tile, (j + 1) * tile)
                res = dot(left, d_ref[:, cols]) + got[:, cols].astype(F32)
                outs[h * 2 + i][:, cols] = res.astype(BF16)


def grad_down_body(tile, ids, h_ref, c_ref, got_ref, first_ref, second_ref, mine_ref):
    units, half = mine_ref.shape
    cut = half // 2
    for k in range(units // tile):
        place = pl.multiple_of((ids[0] & 1) * units + k * tile, tile)
        left = h_ref[:, pl.ds(place, tile)].T
        rows = slice(k * tile, (k + 1) * tile)
        for i in range(2):
            cols = pl.ds(pl.multiple_of(((1 - i) ^ ids[2]) * half, half), half)
            res = (dot(left, c_ref[:, cols]) + got_ref[i, rows, :].astype(F32)).astype(BF16)
            if i == 0:
                first_ref[rows, :] = res[:, :cut]
                second_ref[rows, :] = res[:, cut:]
            else:
                mine_ref[rows, :] = res


def own_body(ids, d_ref, x_ref, branch_ref, cot_ref, gain_ref, dres_ref, low_ref, part_ref):
    resid = x_ref[...].astype(F32) + branch_ref[...].astype(F32)
    r2 = inv_rms(resid)
    n2 = resid * r2
    d = d_ref[...].astype(F32)
    u = d * gain_ref[1:2, :]
    d_resid = cot_ref[...].astype(F32) + r2 * (u - n2 * jnp.mean(u * n2, axis=-1, keepdims=True))
    dres_ref[...] = d_resid
    low_ref[...] = d_resid.astype(BF16)
    part_ref[...] = jnp.broadcast_to(jnp.sum(d * n2, axis=0, keepdims=True), part_ref.shape)


def attend_back_body(n_row, n_col, heads, ids, *refs):
    q_ref, own_ref, oth_ref, lo_ref, hi_ref, l_ref, cos_ref, sin_ref = refs[:8]
    refs = refs[8:]
    db_ref, w_ref, dq_ref, out_ref, kv_own, kv_oth, dm_ref = refs
    dm_ref[...] = dot_nt(db_ref[...], w_ref[...]).astype(BF16)
    col = ids[2]
    n = q_ref.shape[0] // n_row
    kv_own[...] = jnp.zeros_like(kv_own)
    kv_oth[...] = jnp.zeros_like(kv_oth)
    for r in range(n_row):
        rows = slice(r * n, (r + 1) * n)
        count = (r + 1) * n
        q = stack_heads(q_ref[rows, :], heads)
        dm = stack_heads(dm_ref[rows, :], heads)
        lo = jnp.concatenate([lo_ref[rows, :]] * heads, axis=0)
        hi = jnp.concatenate([hi_ref[rows, :]] * heads, axis=0)
        log_total = jnp.concatenate([l_ref[rows, h : h + 1] for h in range(heads)], axis=0)
        oks = key_masks(lo, hi, count, n, n_col, col)
        probs, d_probs = [], []
        for ok, kv_ref in zip(oks, (own_ref, oth_ref)):
            scores = dot_nt(q, kv_ref[:count, :HEAD])
            probs.append(jnp.where(ok, jnp.exp(jnp.where(ok, scores - log_total, NEG_FILL)), 0.0))
            d_probs.append(dot_nt(dm, kv_ref[:count, HEAD:]))
        mean = jnp.sum(probs[0] * d_probs[0], axis=-1, keepdims=True) + jnp.sum(
            probs[1] * d_probs[1], axis=-1, keepdims=True
        )
        dq = None
        for p, dpr, kv_ref, acc in zip(probs, d_probs, (own_ref, oth_ref), (kv_own, kv_oth)):
            ds = (p * (dpr - mean)).astype(BF16)
            part = dot(ds, kv_ref[:count, :HEAD])
            dq = part if dq is None else dq + part
            acc[:count, :HEAD] += dot_tn(ds, q)
            acc[:count, HEAD:] += dot_tn(p.astype(BF16), dm)
        cos_part, sin_part = cos_ref[rows, :], sin_ref[rows, :]
        for h in range(heads):
            piece = turn(dq[h * n : (h + 1) * n], cos_part, -sin_part) * SCALE
            dq_ref[rows, h * HEAD : (h + 1) * HEAD] = piece.astype(BF16)
    for r in range(n_row):
        rows = slice(r * n, (r + 1) * n)
        out_ref[r * n_col + col] = kv_own[rows, :].astype(BF16)
        out_ref[r * n_col + 1 - col] = kv_oth[rows, :].astype(BF16)


def keyval_body(ids, cos_ref, sin_ref, pieces_ref, out_ref):
    total = jnp.sum(pieces_ref[...].astype(F32), axis=0)
    out_ref[:, :HEAD] = turn(total[:, :HEAD], cos_ref[...], -sin_ref[...]).astype(BF16)
    out_ref[:, HEAD:] = total[:, HEAD:].astype(BF16)


def deal_rows(n_row, n_col, shard, ids, res, line_of, send_ref, keep_ref):
    step = pl.program_id(0)
    other = (step & 1) == 0
    for r in range(n_row):
        for c in range(n_col):
            k = r * n_col + c
            block = res[k * shard : (k + 1) * shard]
            if line_of is not None:
                line = lax.broadcasted_iota(jnp.int32, (16, res.shape[1]), 0)
                wide = jnp.broadcast_to(line_of(k), (16, res.shape[1]))
                pad = jnp.where(line == 0, wide, 0.0).astype(BF16)
                block = jnp.concatenate([block, pad], axis=0)
            tall = block.shape[0]
            spot = (step // 2) * n_col + c

            @pl.when(other)
            def _():
                send_ref[spot, r * tall : (r + 1) * tall, :] = block

            @pl.when(jnp.logical_not(other))
            def _():
                keep_ref[spot, r * tall : (r + 1) * tall, :] = block


def project_out_body(n_dp, n_col, ids, mixed_ref, db_ref, send_ref, keep_ref, scr):
    scr[...] = mixed_ref[...].T
    shard = send_ref.shape[1]
    rows = n_col * shard
    for y in range(n_dp // 2):
        for flip, out in ((1, send_ref), (0, keep_ref)):
            place = pl.multiple_of((y * 2 + ((ids[0] & 1) ^ flip)) * rows, rows)
            res = dot(scr[pl.ds(place, rows), :], db_ref[...]).astype(BF16)
            for c in range(n_col):
                out[y * n_col + c] = res[c * shard : (c + 1) * shard]


def project_in_body(n_row, n_col, shard, ids, left_ref, dq_ref, dkv_ref, gain_ref, *refs):
    send_ref, keep_ref, scr = refs
    scr[...] = left_ref[...].T
    n = dkv_ref.shape[0]
    own = scr[:, pl.ds(pl.multiple_of(ids[1] * n, n), n)]
    res = jnp.concatenate(
        [dot(scr[...], dq_ref[...]).astype(BF16), dot(own, dkv_ref[...]).astype(BF16)], axis=1
    )
    deal_rows(
        n_row, n_col, shard, ids, res, lambda k: gain_ref[k : k + 1, :], send_ref, keep_ref
    )


def attn_grad_body(ids, d_ref, w_ref, out_ref):
    out_ref[...] = dot_nt(d_ref[...], w_ref[:, : d_ref.shape[1]]).astype(BF16)


def token_body(ids, d_ref, dkv_ref, wkv_ref, x_ref, gain_ref, dres_ref, out_ref):
    d = d_ref[...].astype(F32) + dot_nt(dkv_ref[...], wkv_ref[:, wkv_ref.shape[1] - 2 * HEAD :])
    x = x_ref[...].astype(F32)
    r1 = inv_rms(x)
    n1 = x * r1
    u = d * gain_ref[0:1, :]
    out = dres_ref[...] + r1 * (u - n1 * jnp.mean(u * n1, axis=-1, keepdims=True))
    out_ref[...] = out.astype(BF16)


def last_body(n_row, hcols, ids, pieces_ref, wq_ref, wkv_ref, gain_ref, *refs):
    gq_ref, gkv_ref, ga_ref, gf_ref = refs
    shard = gq_ref.shape[0]
    gkv = jnp.sum(pieces_ref[:, :shard, hcols:].astype(F32), axis=0)
    gkv_ref[...] = gkv
    gf_ref[...] = jnp.sum(pieces_ref[:, shard:, :].astype(F32), axis=0)[:8]
    total = jnp.sum(gkv * wkv_ref[...].astype(F32), axis=-1, keepdims=True)
    for r in range(n_row):
        cols = slice(r * hcols, (r + 1) * hcols)
        part = pieces_ref[r, :shard, :hcols].astype(F32)
        gq_ref[:, cols] = part
        total = total + jnp.sum(part * wq_ref[:, cols].astype(F32), axis=-1, keepdims=True)
    ga_ref[...] = total / gain_ref[...]


def join_body(ids, mine_ref, rest_ref, out_ref):
    rows = out_ref.shape[0]
    count = mine_ref.shape[0] // rows
    step = pl.program_id(0)
    place = pl.ds(pl.multiple_of((step % count) * rows, rows), rows)
    mine = (ids[0] & 1) == step // count

    @pl.when(mine)
    def _():
        out_ref[...] = mine_ref[place, :].astype(F32)

    @pl.when(jnp.logical_not(mine))
    def _():
        out_ref[...] = rest_ref[place, :].astype(F32)


def join_four_body(ids, own_ref, other_ref, own_rest_ref, other_rest_ref, out_ref):
    step = pl.program_id(0)
    core, y = ids[0] & 1, ids[0] // 2
    for flip, parts in ((0, (own_ref, other_ref)), (1, (own_rest_ref, other_rest_ref))):
        for k, part in enumerate(parts):

            @pl.when(step == (core ^ flip) * 2 + (y ^ k))
            def _():
                out_ref[...] = part[...].astype(F32)


def layout(length_row, order_row, where_at):
    slot_ids = jnp.arange(length_row.shape[0], dtype=jnp.int32)
    placed = jnp.sum(
        jnp.where(order_row[:, None] == slot_ids[None, :], length_row[None, :], 0),
        axis=1,
        dtype=jnp.int32,
    )
    before = jnp.where(slot_ids[None, :] < slot_ids[:, None], placed[None, :], 0)
    starts = jnp.sum(before, axis=1, dtype=jnp.int32)
    ends = starts + placed
    within = (where_at[:, None] >= starts[None, :]) & (where_at[:, None] < ends[None, :])
    begin = jnp.sum(jnp.where(within, starts[None, :], 0), axis=1, dtype=jnp.int32)
    return jnp.where(where_at < jnp.sum(placed), where_at - begin, 0)


def add_body(ids, left_ref, right_ref, out_ref):
    out_ref[...] = (left_ref[...].astype(F32) + right_ref[...].astype(F32)).astype(BF16)


def three_body(ids, a_ref, b_ref, c_ref, out_ref):
    total = a_ref[...].astype(F32) + b_ref[...].astype(F32) + c_ref[...].astype(F32)
    out_ref[...] = total.astype(BF16)


def beside_body(ids, left_ref, first_ref, second_ref, out_ref):
    cut = first_ref.shape[1]
    for k, part in enumerate((first_ref, second_ref)):
        cols = slice(k * cut, (k + 1) * cut)
        total = left_ref[:, cols].astype(F32) + part[...].astype(F32)
        out_ref[:, cols] = total.astype(BF16)


def tile_of(size, wanted):
    while size % wanted:
        wanted //= 2
    return wanted


def shards(
    tokens,
    cotangent,
    w_query,
    w_keyval,
    w_out,
    norm_attn,
    norm_ffn,
    w_gate,
    w_up,
    w_down,
    lengths,
    placement,
):
    n_y, n_row, n_col = lax.axis_size("y"), lax.axis_size("row"), lax.axis_size("col")
    n_dp = 2 * n_y
    dp, row, col = lax.axis_index(DP), lax.axis_index("row"), lax.axis_index("col")
    ids = jnp.stack([dp, row, col]).astype(jnp.int32)
    n, width = tokens.shape
    half = width // n_col
    rows_all = n_row * n
    heads = HEADS // n_row
    hcols = heads * HEAD
    part = width // n_row
    shard = w_query.shape[0]
    ffn = w_gate.shape[1]
    chunk = half // n_dp
    used = hcols + 2 * HEAD
    tall = shard + 16

    def add_low(left, right):
        return run(add_body, ids, [left, right], [None, None], [sds(left.shape)], [None])[0]

    zeros = jnp.zeros((1, used - shard), BF16)
    pack = run(
        functools.partial(pack_body, n_row),
        ids,
        [w_query, w_keyval]
        + [jnp.concatenate([g[None, :], zeros], axis=1) for g in (norm_attn, norm_ffn)],
        [None] * 4,
        [sds((n_row, tall, used))],
        [None],
    )[0]
    packed = deal(pack, "row").reshape(1, n_row * tall, used)
    x_low = lax.all_gather(tokens, "row", axis=0, tiled=True)
    wo_turned = transpose_devices(after(w_out, packed))[None]
    around = n_y * n_col
    pack_own = deal(jnp.broadcast_to(packed, (around,) + packed.shape[1:]), ("y", "col"))
    pack_oth = swap_core(pack_own)
    cot = lax.all_gather(after(cotangent, pack_own), "row", axis=0, tiled=True)

    where_at = (
        (jnp.arange(n_row, dtype=jnp.int32) * (n_col * n))[:, None]
        + jnp.arange(n, dtype=jnp.int32)
        + col * n
    ).reshape(-1)
    offset = layout(lengths[0], placement[0], where_at)
    low_at, high_at = (where_at - offset)[:, None], where_at[:, None]
    frequency = ROPE_BASE ** (-2.0 * jnp.arange(HEAD // 2, dtype=jnp.int32).astype(F32) / HEAD)
    angle = offset.astype(F32)[:, None] * frequency[None, :]
    cos_part, sin_part = jnp.cos(angle), jnp.sin(angle)
    cos_all = jnp.concatenate([cos_part, cos_part], axis=1)
    sin_all = jnp.concatenate([-sin_part, sin_part], axis=1)

    attn_in, kv_own, query, w_qkv, gains = run(
        functools.partial(front_body, n_row, n_col, hcols, shard),
        ids,
        [x_low, pack_own, pack_oth, cos_all, sin_all],
        [None, None, None, None, None],
        [
            sds((rows_all, width)),
            sds((rows_all, 2 * HEAD)),
            sds((rows_all, hcols)),
            sds((width, used)),
            sds((8, width), F32),
        ],
        [None, None, None, None, None],
        scratch=[pltpu.VMEM((width // shard, HEAD), F32)] * 2,
    )
    kv_oth = swap_col(kv_own)
    wo_own = deal(
        jnp.broadcast_to(after(wo_turned, kv_own), (around,) + wo_turned.shape[1:]),
        ("y", "col"),
    )
    mixed, log_total = run(
        functools.partial(attend_body, n_row, n_col, heads),
        ids,
        [query, kv_own, kv_oth, low_at, high_at],
        [None] * 5,
        [sds((rows_all, hcols)), sds((rows_all, HEAD), F32)],
        [None] * 2,
    )
    wo_oth = swap_core(after(wo_own, mixed))
    gate_cut, up_cut, down_cut = run(
        cut_body,
        ids,
        [w_gate, w_up, after(w_down, mixed)],
        [pl.BlockSpec((chunk, ffn), lambda i, ids: (ids[0], 0))] * 2
        + [pl.BlockSpec((ffn, chunk), lambda i, ids: (0, ids[0]))],
        [sds((chunk, ffn))] * 2 + [sds((ffn, chunk))],
        [None] * 3,
    )
    gate_got = swap_col(gate_cut)
    up_got = swap_col(after(up_cut, gate_got))
    down_got = swap_col(after(down_cut, up_got))
    gate_y = [gate_got] + [swap_y(gate_got, k) for k in range(1, n_y)]
    up_y = [up_got] + [swap_y(up_got, k) for k in range(1, n_y)]
    down_y = [down_got] + [swap_y(down_got, k) for k in range(1, n_y)]
    part_branch, w_rows = run(
        functools.partial(branch_body, n_col),
        ids,
        [mixed, wo_own, wo_oth],
        [None, None, None],
        [sds((rows_all, width)), sds((hcols, width))],
        [None] * 2,
    )
    branch = lax.psum_scatter(after(part_branch, cot), "row", scatter_dimension=0, tiled=True)
    ffn_own_in = run(
        norm_body,
        ids,
        [tokens, after(branch, up_got, *gate_y), gains],
        [None] * 3,
        [sds((n, width))],
        [None],
    )[0]
    ffn_in = lax.all_gather(ffn_own_in, "row", axis=0, tiled=True)

    def with_core(own, around_y):
        return [own] + [x for g in around_y for x in (g, swap_core(after(g, part_branch)))]

    gates, ups, downs = (
        with_core(w_gate, gate_y),
        with_core(w_up, up_y),
        with_core(w_down, down_y),
    )

    tile = tile_of(ffn, 512)
    tiles = ffn // tile
    quarter = half // 2

    def at(j):
        return jnp.minimum(j, tiles - 1)

    def once(array):
        zeros = (0,) * len(array.shape)
        return pl.BlockSpec(array.shape, lambda *_: zeros, pipeline_mode=pl.Buffered(1))

    into = [pl.BlockSpec((half, tile), lambda j, ids: (0, at(j)))] + [
        pl.BlockSpec((chunk, tile), lambda j, ids: (0, at(j)))
    ] * n_dp
    late = lambda j, ids: (jnp.maximum(j - tiles, 0), 0, 0)
    hidden, d_gate, d_up, d_ffn, sent_down, sent_gate, sent_up = run(
        functools.partial(ffn_body, n_dp, tiles),
        ids,
        [ffn_in, cot] + gates + ups + downs,
        [once(ffn_in), once(cot)]
        + into * 2
        + [pl.BlockSpec((tile, half), lambda j, ids: (at(j), 0))]
        + [pl.BlockSpec((tile, chunk), lambda j, ids: (at(j), 0))] * n_dp,
        [sds((rows_all, ffn))] * 3
        + [sds((rows_all, width)), sds((2, ffn // 2, half))]
        + [sds((2, quarter, ffn))] * 2,
        [pl.BlockSpec((rows_all, tile), lambda j, ids: (0, at(j)))] * 3
        + [None, pl.BlockSpec((1, ffn // 2, half), late)]
        + [pl.BlockSpec((1, quarter, ffn), late)] * 2,
        grid=(tiles + 2,),
        scratch=[pltpu.VMEM((rows_all, width), F32)]
        + [pltpu.VMEM((rows_all, ffn), BF16)] * 3
        + [pltpu.VMEM((width, 2 * tile), BF16), pltpu.VMEM((tile, width), BF16)],
        limit=60,
    )
    d_own = lax.psum_scatter(d_ffn, "row", scatter_dimension=0, tiled=True)

    ft = tile_of(ffn, 512)
    rt = tile_of(ffn // 2, 256)

    def grad_in(right, got, *gate_on):
        body = functools.partial(grad_in_body, ft)
        args = [after(ffn_in, *gate_on), right, got]
        return run(body, ids, args, [None] * 3, [sds((quarter, ffn))] * 2, [None] * 2)

    def grad_in_y(right, got, *gate_on):
        return run(
            functools.partial(grad_in_y_body, ft),
            ids,
            [after(ffn_in, *gate_on), right, got],
            [None, None, None],
            [sds((quarter // 2, ffn))] * 4,
            [None] * 4,
        )

    def grad_down_part(got, *gate_on):
        body = functools.partial(grad_down_body, rt)
        args = [after(hidden, *gate_on), cot, got]
        outs = [sds((ffn // 2, half // 2))] * 2 + [sds((ffn // 2, half))]
        return run(body, ids, args, [None] * 3, outs, [None] * 3)

    got_down = swap_core(sent_down)
    got_gate = swap_core(sent_gate)
    got_up = swap_core(sent_up)
    theirs_first, theirs_second, mine_down = grad_down_part(got_down, d_ffn)
    col_first = swap_col(theirs_first)
    if n_y == 2:
        send_theirs, send_mine, keep_theirs, keep_mine = grad_in_y(d_gate, got_gate, theirs_first)
        y_theirs = swap_y(send_theirs, 1)
        early = [col_first, y_theirs]
    else:
        theirs_gate, keep_mine = grad_in(d_gate, got_gate, theirs_first)
        early = [col_first]
    ffn_out = run(
        functools.partial(down_body, n_dp),
        ids,
        [after(hidden, keep_mine)] + downs,
        [None] * (2 + n_dp),
        [sds((rows_all, width))],
        [None],
    )[0]

    d_resid, d_low, gain_part = run(
        own_body,
        ids,
        [after(d_own, ffn_out), tokens, branch, cotangent, gains],
        [None] * 5,
        [sds((n, width), F32), sds((n, width)), sds((8, width), F32)],
        [None] * 3,
    )
    d_branch = lax.all_gather(after(d_low, *early), "row", axis=0, tiled=True)
    ffn_own = lax.psum_scatter(after(ffn_out, d_low, *early), "row", scatter_dimension=0, tiled=True)

    def y_total(value, *others):
        total = value
        step = 1
        while step < n_y:
            total = add_low(total, after(swap_y(total, step), *others))
            step *= 2
        return total

    def three(a, b, c):
        return run(three_body, ids, [a, b, c], [None] * 3, [sds(a.shape)], [None])[0]

    col_second = swap_col(after(theirs_second, col_first, d_low))
    if n_y == 2:
        y_mine = swap_y(after(send_mine, y_theirs, d_low), 1)
        theirs_gate = add_low(keep_theirs, after(y_theirs, d_low))
    col_gate = swap_col(theirs_gate)
    theirs_up, mine_up = grad_in(d_up, got_up, d_low, theirs_gate)
    sum_down = run(
        beside_body,
        ids,
        [mine_down, col_first, after(col_second, theirs_gate)],
        [None] * 3,
        [sds(mine_down.shape)],
        [None],
    )[0]
    col_up = swap_col(after(theirs_up, col_gate))
    if n_y == 2:
        moved_down = swap_y(sum_down, 1)
        sum_gate = three(keep_mine, y_mine, col_gate)
        full_gate = swap_y(sum_gate, 1)
    else:
        moved_down = sum_down
        sum_gate = add_low(keep_mine, col_gate)
        full_gate = y_total(sum_gate)

    d_query, d_kv_parts = run(
        functools.partial(attend_back_body, n_row, n_col, heads),
        ids,
        [query, kv_own, kv_oth, low_at, high_at, log_total, cos_all, sin_all]
        + [after(d_branch, sum_gate, theirs_up, sum_down), w_rows],
        [None] * 10,
        [sds((rows_all, hcols)), sds((n_row * n_col, n, 2 * HEAD))],
        [None] * 2,
        scratch=[pltpu.VMEM((rows_all, 2 * HEAD), F32)] * 2
        + [pltpu.VMEM((rows_all, hcols), BF16)],
    )
    d_kv_parts = deal(d_kv_parts, ("row", "col"))
    d_attn = run(
        attn_grad_body, ids, [after(d_query, moved_down, col_up, full_gate), w_qkv], [None] * 2, [sds((rows_all, width))], [None]
    )[0]
    d_attn_own = lax.psum_scatter(d_attn, "row", scatter_dimension=0, tiled=True)

    result = (tokens.astype(F32) + branch.astype(F32) + ffn_own.astype(F32)).astype(BF16)
    mine = lax.dynamic_slice_in_dim(result, col * half, half, 1)
    moved = swap_col(lax.dynamic_slice_in_dim(result, (1 - col) * half, half, 1))
    result = jnp.where(
        col == 0, jnp.concatenate([mine, moved], axis=0), jnp.concatenate([moved, mine], axis=0)
    )

    by_dp = width // n_dp

    def block_of(j, ids):
        return (j // 2) * 2 + ((ids[0] & 1) ^ ((j & 1) ^ 1))

    lines = n_row * n_col
    gain_lines = jnp.pad(
        gain_part[0].reshape(n_dp * lines, shard), ((0, 0), (0, used - shard))
    )
    own_cos = lax.dynamic_slice_in_dim(cos_all, row * n, n, 0)
    own_sin = lax.dynamic_slice_in_dim(sin_all, row * n, n, 0)
    d_kv = run(
        keyval_body,
        ids,
        [own_cos, own_sin, after(d_kv_parts, d_attn)],
        [None, None, None],
        [sds((n, 2 * HEAD))],
        [None],
    )[0]
    send_q, keep_q = run(
        functools.partial(project_in_body, n_row, n_col, shard),
        ids,
        [attn_in, d_query, d_kv, gain_lines],
        [
            pl.BlockSpec((rows_all, by_dp), lambda j, ids: (0, block_of(j, ids))),
            None,
            None,
            pl.BlockSpec((lines, used), lambda j, ids: (block_of(j, ids), 0)),
        ],
        [sds((around, n_row * tall, used))] * 2,
        [None] * 2,
        grid=(n_dp,),
        scratch=[pltpu.VMEM((by_dp, rows_all), BF16)],
    )
    got_q = swap_core(send_q)
    if n_y == 2:
        full_down = add_low(sum_down, after(moved_down, send_q))
        sum_up = add_low(mine_up, after(col_up, full_down))
        moved_up = swap_y(sum_up, 1)
    else:
        full_down = y_total(sum_down)
        sum_up = moved_up = add_low(mine_up, after(col_up, full_down, full_gate))
    send_o, keep_o = run(
        functools.partial(project_out_body, n_dp, n_col),
        ids,
        [mixed, after(d_branch, sum_up)],
        [None] * 2,
        [sds((around, shard, width))] * 2,
        [None] * 2,
        scratch=[pltpu.VMEM((hcols, rows_all), BF16)],
    )
    o_total = keep_o.astype(F32) + swap_core(send_o).astype(F32)
    o_total = o_total.astype(BF16).reshape(n_y, n_col, shard, width)

    def pick(value, which, axis):
        return lax.dynamic_index_in_dim(value, which, axis, keepdims=False)

    o_theirs = swap_col(pick(o_total, 1 - col, 1))

    def parts_sum(total, *others):
        dealt = after(deal(total, ("y", "col")), *others)
        return jnp.sum(dealt.astype(F32), axis=0).astype(BF16)

    q_total = (keep_q.astype(F32) + after(got_q, full_down).astype(F32)).astype(BF16)
    def joined(mine, shape):
        return run(
            join_body,
            ids,
            [mine, swap_core(mine)],
            [None] * 2,
            [sds(shape, F32)],
            [pl.BlockSpec((shape[0] // 4, shape[1]), lambda b, ids: (b, 0))],
            grid=(4,),
        )[0]

    grad_down = joined(after(full_down, got_q), (ffn, half))
    def join_four(parts):
        return run(
            join_four_body,
            ids,
            parts + [swap_core(p) for p in parts],
            [None] * 4,
            [sds((half, ffn), F32)],
            [pl.BlockSpec((half // 4, ffn), lambda b, ids: (b, 0))],
            grid=(4,),
        )[0]

    if n_y == 2:
        grad_gate = join_four([sum_gate, after(full_gate, grad_down)])
    else:
        grad_gate = joined(full_gate, (half, ffn))

    grad_tokens = run(
        token_body,
        ids,
        [d_attn_own, d_kv, w_qkv, tokens, gains, d_resid],
        [None] * 6,
        [sds((n, width))],
        [None],
    )[0]

    q_sum = parts_sum(q_total, grad_down, grad_gate, grad_tokens, result, moved_up, o_theirs)
    if n_y == 2:
        full_up = add_low(sum_up, after(moved_up, q_sum))
    else:
        full_up = y_total(sum_up, q_sum)
    q_pieces = deal(q_sum.reshape(n_row, tall, used), "row")
    o_both = (pick(o_total, col, 1).astype(F32) + o_theirs.astype(F32)).astype(BF16)
    y = lax.axis_index("y")
    o_own = pick(o_both, y, 0).astype(F32)
    for k in range(1, n_y):
        o_own = o_own + swap_y(pick(o_both, y ^ k, 0), k).astype(F32)
    grad_out = transpose_devices(o_own.astype(BF16)).astype(F32)
    grad_up = joined(full_up, (half, ffn))
    grad_query, grad_keyval, gain_a, gain_f = run(
        functools.partial(last_body, n_row, hcols),
        ids,
        [after(q_pieces, grad_up), w_query, w_keyval, norm_attn.astype(F32)[:, None]],
        [None, None, None, None],
        [
            sds((shard, width), F32),
            sds((shard, 2 * HEAD), F32),
            sds((shard, 1), F32),
            sds((8, used), F32),
        ],
        [None] * 4,
    )
    return (
        result,
        grad_tokens,
        grad_query,
        grad_keyval,
        grad_out,
        gain_a[:, 0],
        gain_f[0, :shard],
        grad_gate,
        grad_up,
        grad_down,
    )


def solution(mesh):
    n_dp, n_row, n_col = (mesh.shape[a] for a in ("dp", "row", "col"))
    fine = jax.sharding.Mesh(mesh.devices.reshape(n_dp // 2, 2, n_row, n_col), EVERY)
    rows = P(EVERY, None)
    in_specs = (
        rows,
        rows,
        rows,
        rows,
        rows,
        P(EVERY),
        P(EVERY),
        P("col", "row"),
        P("col", "row"),
        P("row", "col"),
        P(DP, None),
        P(DP, None),
    )
    out_specs = (
        P(DP + ("row",), "col"),
        rows,
        rows,
        rows,
        rows,
        P(EVERY),
        P(EVERY),
        P("col", "row"),
        P("col", "row"),
        P("row", "col"),
    )
    return jax.shard_map(shards, mesh=fine, in_specs=in_specs, out_specs=out_specs, check_vma=False)
```
